128 devices in a mesh: aux: 16 (over z, x_lo, core), pair: 8 (over x_hi, y).
Axes of the slice: x: 4 (x_hi: 2, x_lo: 2; x = x_hi * 2 + x_lo), y: 4, z: 4, core: 2. Of those that a mesh axis runs over, the one named last changes fastest.
Arguments:
- coeffs: bfloat16 [12288, 49152], P('aux', 'pair'), may hold values from -0.0390625 to 0.0390625
- occ_index: int32 [49152], P('pair'), may hold values from 0 to 4095
- virt_index: int32 [49152], P('pair'), may hold values from 0 to 32767
- occ_energy: float32 [4096], replicated, may hold values from -1.5 to -0.25
- virt_energy: float32 [32768], replicated, may hold values from 0.02 to 3
Outputs:
- band: float32 [7, 12288, 768], P(None, ('aux', 'pair'))
The draws below stay inside these ranges and needn't reach their ends.
All inputs are finite; a program needn't handle non-finite values.
Results may differ from the reference program's by a relative error of at most 0.0011.
Values may be sent and summed in bfloat16 or wider, within the bound.
No kernel may reach another device: no remote copies, remote signals or barrier semaphores. Data moves between devices by JAX's collectives and lax.ppermute only.
A program may use at most 128 MiB of HBM per device.

```python
import math
import jax
import jax.numpy as jnp
from jax import lax

NAUX = 12288
NOCC = 4096
NVIRT = 32768
STEPS = 4
AUX_DEV = 768
NPAIR = 49152
N_AUX = 16


def touch_ends(drawn, stream_key, smallest, top_value):
    spot = [jax.random.randint(jax.random.fold_in(stream_key, axis), (), 0, length) for axis, length in enumerate(drawn.shape)]
    main_axis = drawn.shape.index(max(drawn.shape))
    neighbour = spot[:main_axis] + [(spot[main_axis] + 1) % drawn.shape[main_axis]] + spot[main_axis + 1:]
    return drawn.at[tuple(spot)].set(smallest).at[tuple(neighbour)].set(top_value)


def with_spikes(drawn, own_key, source, target, parts, factor):
    def block_of(dim):
        return (jnp.arange(drawn.shape[dim]) // (drawn.shape[dim] // parts)).reshape((-1,) + (1,) * (drawn.ndim - 1 - dim))

    first = jax.random.permutation(own_key, parts)[block_of(target)]
    far = (block_of(target) + parts // 2) % parts
    return jnp.where((block_of(source) == first) | (block_of(source) == far), factor * drawn, drawn)


def shard_levels(own_key, dims, shards, least, high):
    def one(dim, blocks):
        draws = jax.random.uniform(jax.random.fold_in(jax.random.fold_in(own_key, 6), dim), (blocks,), jnp.float32, least / len(shards), high / len(shards))
        return jnp.repeat(jnp.exp(draws), dims[dim] // blocks).reshape((-1,) + (1,) * (len(dims) - dim - 1))

    factor_of = one(*shards[0])
    for cut in shards[1:]:
        factor_of = factor_of * one(*cut)
    return factor_of


def gaussian_with(stream_key, shape, deviation, bound, cuts, heavy, kind=jnp.bfloat16):
    drawn = deviation * jax.random.normal(stream_key, shape, jnp.float32)
    if cuts:
        drawn = drawn * shard_levels(stream_key, shape, cuts, -0.22, 0.18)
    return jnp.clip(with_spikes(drawn, jax.random.fold_in(stream_key, 3), *heavy), -bound, bound).astype(kind)


def setup_inputs(seed: int = 0) -> dict:
    seeds = jax.random.split(jax.random.key(seed), 6)
    return {
        "coeffs": gaussian_with(seeds[0], (NAUX, NPAIR), NPAIR ** -0.5, 0.0390625, ((0, 16), (1, 8)), (1, 0, 16, 2.0)),
        "occ_index": touch_ends(jax.random.randint(seeds[1], (NPAIR,), 0, NOCC), jax.random.fold_in(seeds[1], 1), 0, NOCC - 1).astype(jnp.int32),
        "virt_index": touch_ends(jax.random.randint(seeds[2], (NPAIR,), 0, NVIRT), jax.random.fold_in(seeds[2], 1), 0, NVIRT - 1).astype(jnp.int32),
        "occ_energy": jnp.clip(jax.random.uniform(seeds[3], (NOCC,), jnp.float32, -1.5, -0.25), -1.5, -0.25),
        "virt_energy": jnp.clip(jnp.exp(jax.random.uniform(seeds[4], (NVIRT,), jnp.float32, math.log(0.02), math.log(3.0))), 0.02, 3.0),
    }


freq_point = 0.5


def pair_weights(occ_index, virt_index, occ_energy, virt_energy):
    gap = virt_energy[virt_index] - occ_energy[occ_index]
    return 4.0 * gap / (gap * gap + freq_point * freq_point)


def reference(coeffs, occ_index, virt_index, occ_energy, virt_energy):
    weight = pair_weights(occ_index, virt_index, occ_energy, virt_energy)
    scaled = (coeffs.astype(jnp.float32) * weight[None, :]).astype(jnp.bfloat16)
    blocks = coeffs.reshape(N_AUX, AUX_DEV, NPAIR)
    scaled_blocks = scaled.reshape(N_AUX, AUX_DEV, NPAIR)

    def row_tiles(index):
        left = scaled_blocks[index].astype(jnp.float32)
        result = []
        for offset in range(STEPS):
            other = blocks[(index - offset) % N_AUX].astype(jnp.float32)
            result.append(-jnp.dot(left, other.T, preferred_element_type=jnp.float32))
        return jnp.stack(result)

    lower = lax.map(row_tiles, jnp.arange(N_AUX, dtype=jnp.int32))
    pieces = []
    for offset in range(STEPS - 1, -1, -1):
        pieces.append(lower[:, offset].reshape(NAUX, AUX_DEV))
    for offset in range(1, STEPS):
        moved = jnp.roll(lower[:, offset], -offset, axis=0)
        pieces.append(jnp.swapaxes(moved, 1, 2).reshape(NAUX, AUX_DEV))
    return jnp.stack(pieces)
```

```python
import functools

import jax
import jax.numpy as jnp
import numpy as np
from jax import lax
from jax.experimental import pallas as pl
from jax.experimental.pallas import tpu as pltpu
from jax.sharding import PartitionSpec as P

ROWS = 768
HALF = 3072
PART = 96
PLANES = 4
WIDE = 256
PIECES = 4
DEPTH = HALF // PIECES
freq_point = 0.5

OWN, SIB, FAR_A, FAR_A_SIB, FAR_B, FAR_B_SIB, HALO_A, HALO_B, HALO_A_SIB, HALO_B_SIB, MINOR = range(11)

WHERE = [
    {"A0": OWN, "A1": SIB, "A2": FAR_B, "A3": FAR_A_SIB, "P0": HALO_A, "B3": MINOR},
    {"A1": OWN, "A0": SIB, "A3": FAR_A, "A2": FAR_B_SIB, "P1": HALO_B},
    {"A2": OWN, "A3": SIB, "A0": FAR_A, "A1": FAR_B_SIB, "B2": HALO_B, "B3": HALO_A_SIB, "P0": MINOR},
    {"A3": OWN, "A2": SIB, "A1": FAR_B, "A0": FAR_A_SIB, "B3": HALO_A, "B2": HALO_B_SIB},
]

BATCHES = [
    [["A0A0", "A3A1"],
     ["A1A0", "A1A1"],
     ["A2A2", "A0A0"],
     ["A3A2", "A3A3"]],
    [["P0A1", "P0A3"],
     ["A3A0", "A3A3"],
     ["A0B3", "A2B3"],
     ["A3A0", "A2A0"]],
    [["P0A2", "A2A1"],
     ["P1A2", "P1A3"],
     ["P0A1", "A0B2"],
     ["A1A0", "A1A1"]],
    [["A2A2", "A2B3"],
     ["A3A2", "A2A0"],
     ["A2A1", "A3A1"],
     ["A1B3", "A1B2"]],
]
MOVED = [["A0B1", "A0B3", "A0B2", None], [None, None, "A1B2", "A1B3"],
         [None, None, "A0B1", None], [None, None, None, None]]
ENTRIES = [
    [["A0A0", "A0B3", "A0B2", "A0B1"], ["A2A2", "A2A1", "A3A1", "A2B3"]],
    [["A1A1", "A1A0", "A1B3", "A1B2"], ["A3A3", "A3A2", "A2A0", "A3A0"]],
]
def batch_table(batch, sources):
    return np.array([[sources.index(WHERE[role][tile[at:at + 2]]) for at in (0, 2) for tile in tiles]
                     for role, tiles in enumerate(batch)], np.int32)


def tiles_kernel(count, sources, table, weight, *refs):
    source_refs = refs[:sources]
    out, held, scaled, total, sems = refs[sources:]
    step = pl.program_id(0)
    slot = lax.rem(step, 2)
    here = table[2 * count]

    def copy(k, slot, side, c):
        columns = slice(c * DEPTH, (c + 1) * DEPTH)
        return pltpu.make_async_copy(
            source_refs[k].at[:, columns], held.at[slot, side, :, columns], sems.at[slot, side, c])

    def fetch(tile, slot):
        for c in range(PIECES):
            for side in range(2):
                for k in range(sources):
                    @pl.when(table[side * count + tile] == k)
                    def _():
                        copy(k, slot, side, c).start()

    @pl.when(step == 0)
    def _():
        fetch(0, 0)

    @pl.when(step + 1 < count)
    def _():
        fetch(step + 1, 1 - slot)

    def ready(c):
        columns = slice(c * DEPTH, (c + 1) * DEPTH)
        for side in range(2):
            copy(0, slot, side, c).wait()
        scaled[c % 2] = (held[slot, 0, :, columns].astype(jnp.float32) * weight[:, columns]).astype(jnp.bfloat16)

    ready(0)
    for c in range(PIECES):
        if c + 1 < PIECES:
            ready(c + 1)
        for n in range(ROWS // WIDE):
            columns = slice(n * WIDE, (n + 1) * WIDE)
            acc = lax.dot_general(
                scaled[c % 2], held[slot, 1, columns, c * DEPTH:(c + 1) * DEPTH],
                (((1,), (1,)), ((), ())), preferred_element_type=jnp.float32)
            if c > 0:
                acc = acc + total[:, columns]
            if c + 1 < PIECES:
                total[:, columns] = acc
            else:
                for y in range(4):
                    at = lax.rem(y + 4 - here, 4)
                    for h in range(2):
                        first = (h * 4 + y) * PART
                        out[at, h, 0, :, columns] = acc[first:first + PART]


def tile_batch(table_row, weight, sources):
    count = (table_row.shape[0] - 1) // 2
    return pl.pallas_call(
        functools.partial(tiles_kernel, count, len(sources)),
        grid_spec=pltpu.PrefetchScalarGridSpec(
            num_scalar_prefetch=1,
            grid=(count,),
            in_specs=[pl.BlockSpec((1, HALF), lambda i, t: (0, 0))]
            + [pl.BlockSpec(memory_space=pl.ANY)] * len(sources),
            out_specs=pl.BlockSpec((4, 2, 1, PART, ROWS), lambda i, t: (0, 0, i, 0, 0)),
            scratch_shapes=[
                pltpu.VMEM((2, 2, ROWS, HALF), jnp.bfloat16),
                pltpu.VMEM((2, ROWS, DEPTH), jnp.bfloat16),
                pltpu.VMEM((ROWS, ROWS), jnp.float32),
                pltpu.SemaphoreType.DMA((2, 2, PIECES)),
            ],
        ),
        out_shape=jax.ShapeDtypeStruct((4, 2, count, PART, ROWS), jnp.float32),
        compiler_params=pltpu.CompilerParams(
            dimension_semantics=("arbitrary",), vmem_limit_bytes=44 * 1024 * 1024),
        cost_estimate=pl.CostEstimate(
            flops=count * ROWS * ROWS,
            bytes_accessed=count * ROWS * ROWS,
            transcendentals=0),
    )(table_row, weight, *sources)


def lookup(table, index):
    blocks = table.shape[0]
    high = lax.shift_right_logical(index, 7)
    low = jnp.bitwise_and(index, 127)
    pairs = index.shape[1]
    hot = jnp.where(lax.broadcasted_iota(jnp.int32, (blocks, pairs), 0) == high, 1.0, 0.0).astype(jnp.bfloat16)
    rest = table
    column = jnp.zeros((128, pairs), jnp.float32)
    for _ in range(3):
        piece = rest.astype(jnp.bfloat16)
        rest = rest - piece.astype(jnp.float32)
        column = column + lax.dot_general(
            piece, hot, (((0,), (0,)), ((), ())), preferred_element_type=jnp.float32)
    mask = lax.broadcasted_iota(jnp.int32, (128, pairs), 0) == low
    return jnp.sum(jnp.where(mask, column, 0.0), axis=0, keepdims=True)


def gap_kernel(occ_index, virt_index, occ_energy, virt_energy, gap):
    gap[...] = lookup(virt_energy[...], virt_index[...]) - lookup(occ_energy[...], occ_index[...])


def pair_gaps(occ_index, virt_index, occ_energy, virt_energy):
    block = 512
    pairs = occ_index.shape[0]
    occ_table = occ_energy.reshape(-1, 128)
    virt_table = virt_energy.reshape(-1, 128)
    line = pl.BlockSpec((1, block), lambda i: (0, i))
    return pl.pallas_call(
        gap_kernel,
        grid=(pairs // block,),
        in_specs=[line, line,
                  pl.BlockSpec(occ_table.shape, lambda i: (0, 0)),
                  pl.BlockSpec(virt_table.shape, lambda i: (0, 0))],
        out_specs=line,
        out_shape=jax.ShapeDtypeStruct((1, pairs), jnp.float32),
        cost_estimate=pl.CostEstimate(flops=6 * 128 * 288 * pairs, bytes_accessed=200000, transcendentals=0),
    )(occ_index[None, :], virt_index[None, :], occ_table, virt_table)


def moves(pairs):
    return [(z * 4 + src, (z + dz) % PLANES * 4 + dst) for z in range(PLANES) for src, dst, dz in pairs]


def aux_permute(value, pairs):
    return lax.ppermute(value, "aux", moves(pairs))


def y_permute(value, by):
    return lax.ppermute(value, "pair", [(h * 4 + y, h * 4 + (y + by) % 4) for h in range(2) for y in range(4)])


def x_permute(value, by):
    perm = []
    for z in range(PLANES):
        for x in range(4):
            to = (x + by) % 4
            for core in range(2):
                for y in range(4):
                    source = (z * 4 + x % 2 * 2 + core) * 8 + x // 2 * 4 + y
                    perm.append((source, (z * 4 + to % 2 * 2 + core) * 8 + to // 2 * 4 + y))
    return lax.ppermute(value, ("aux", "pair"), perm)


def ring_sum(part, permute, narrow, wide):
    count = part(0, 0).shape[0]
    up = permute(narrow(jnp.concatenate([part(2, 0), part(1, 1)])), 1)
    down = permute(narrow(jnp.concatenate([part(2, 1), part(3, 0)])), -1)
    up_more = permute(narrow(part(1, 0) + wide(up[:count])), 1)
    down_more = permute(narrow(part(3, 1) + wide(down[:count])), -1)
    zero = part(0, 0) + wide(down[count:]) + wide(up_more)
    one = part(0, 1) + wide(up[count:]) + wide(down_more)
    return zero, one


def slot_names(role):
    names = []
    for batch in BATCHES:
        names += [(tile, h) for h in range(2) for tile in batch[role]]
    early, late = MOVED[role][:2], MOVED[role][2:]
    names += [(tile, h) for h in range(2) for tile in early]
    names += [(tile, h) for h in range(2) for tile in late]
    return names


def entry_table():
    rows = []
    for role in range(4):
        names = slot_names(role)
        for x_hi in range(2):
            row = []
            for k in range(4):
                to = (x_hi * 2 + role // 2 + k) % 4
                row += [names.index((tile, to // 2)) for tile in ENTRIES[role % 2][to % 2]]
            rows.append(row)
    return np.array(rows, np.int32)


def pick_kernel(table, slots, parts):
    for i in range(16):
        parts[i] = slots[table[i]]


def pick_parts(table, slots):
    return pl.pallas_call(
        pick_kernel,
        in_specs=[pl.BlockSpec(memory_space=pltpu.SMEM), pl.BlockSpec(memory_space=pltpu.VMEM)],
        out_specs=pl.BlockSpec(memory_space=pltpu.VMEM),
        out_shape=jax.ShapeDtypeStruct((16, PART, ROWS), jnp.float32),
        compiler_params=pltpu.CompilerParams(vmem_limit_bytes=20 * 1024 * 1024),
        cost_estimate=pl.CostEstimate(flops=0, bytes_accessed=PART * ROWS, transcendentals=0),
    )(table, slots)


def largest_round(value, permute):
    got = [permute(value, by) for by in (1, 2, 3)]
    return jnp.maximum(jnp.maximum(value, got[0]), jnp.maximum(got[1], got[2]))


def z_permute(value, by):
    return aux_permute(value, [(r, r, by) for r in range(4)])


def after(value, other):
    return lax.optimization_barrier((value, other))[0]


def local(coeffs, occ_index, virt_index, occ_energy, virt_energy):
    role = lax.rem(lax.axis_index("aux"), 4)
    x_lo = role // 2
    x_hi = lax.axis_index("pair") // 4
    y = lax.rem(lax.axis_index("pair"), 4)

    largest = jnp.max(jnp.abs(coeffs).reshape(-1, 8, coeffs.shape[1]), axis=0)
    largest = jnp.max(largest.reshape(8, -1, 128), axis=1).astype(jnp.float32)
    largest = largest_round(largest, x_permute)

    other = lax.dynamic_slice_in_dim(coeffs, (1 - x_lo) * HALF, HALF, axis=1)
    other, largest = lax.optimization_barrier((other, largest))
    far_a = aux_permute(other, [(0, 2, 0), (3, 1, 0)])
    largest = largest_round(largest, z_permute)
    mine = lax.dynamic_slice_in_dim(after(coeffs, other), x_lo * HALF, HALF, axis=1)
    mine, largest = lax.optimization_barrier((mine, largest))
    halo_a = aux_permute(mine, [(0, 0, -1), (3, 3, 1)])
    sib = aux_permute(mine, [(0, 1, 0), (1, 0, 0), (2, 3, 0), (3, 2, 0)])
    far_b = aux_permute(after(other, far_a), [(1, 3, 0), (2, 0, 0)])

    largest = largest_round(largest, y_permute)
    largest = jnp.maximum(largest, aux_permute(largest, [(0, 1, 0), (1, 0, 0), (2, 3, 0), (3, 2, 0)]))
    largest = jnp.max(largest)
    bound = 8.0 * HALF * 4 * largest * largest * 4.0
    scale = 32768.0 / jnp.maximum(bound, 1e-30)
    unscale = 1.0 / scale

    def narrow(value):
        return (value * scale).astype(jnp.float16)

    def wide(value):
        return value.astype(jnp.float32) * unscale

    begin = x_lo * HALF
    gap = pair_gaps(
        lax.dynamic_slice_in_dim(occ_index, begin, HALF),
        lax.dynamic_slice_in_dim(virt_index, begin, HALF),
        occ_energy, virt_energy)
    weight = -4.0 * gap / (gap * gap + freq_point * freq_point)

    plans = []
    for batch in BATCHES:
        used = sorted({WHERE[r][t[i:i + 2]] for r in range(4) for t in batch[r] for i in (0, 2)})
        row = lax.dynamic_index_in_dim(jnp.asarray(batch_table(batch, used)), role, axis=0, keepdims=False)
        row = jnp.concatenate([row, y[None].astype(jnp.int32)])
        plans.append([used, row])
    entries = lax.dynamic_index_in_dim(jnp.asarray(entry_table()), role * 2 + x_hi, axis=0, keepdims=False)
    rows = [plan[1] for plan in plans]
    far_a, scale, unscale, weight, entries, rows = lax.optimization_barrier(
        (far_a, scale, unscale, weight, entries, rows))

    far_a_sib = aux_permute(far_a, [(1, 0, 0), (2, 3, 0)])
    minor = aux_permute(far_a, [(1, 0, 1), (2, 2, -1)])
    halo_a, far_a_sib = lax.optimization_barrier((halo_a, far_a_sib))
    halo_b = aux_permute(after(mine, halo_a), [(1, 1, -1), (2, 2, 1)])
    halo_a_sib = aux_permute(halo_a, [(3, 2, 0)])

    held = {OWN: mine, SIB: sib, FAR_A: far_a, FAR_A_SIB: far_a_sib, HALO_A: halo_a}

    def tiles(number):
        return tile_batch(rows[number], weight, [held[s] for s in plans[number][0]])

    def first_sends(partial):
        return [narrow(jnp.concatenate([partial[2, 0], partial[1, 1]])),
                narrow(jnp.concatenate([partial[2, 1], partial[3, 0]]))]

    def first_round(sends):
        return [y_permute(sends[0], 1), y_permute(sends[1], -1)]

    def second_sends(partial, got):
        return [narrow(partial[1, 0] + wide(got[0][:2])), narrow(partial[3, 1] + wide(got[1][:2]))]

    def finish(partial, got, more):
        zero = partial[0, 0] + wide(got[1][2:]) + wide(more[0])
        one = partial[0, 1] + wide(got[0][2:]) + wide(more[1])
        return [zero, one]

    partial0 = tiles(0)
    sends0 = first_sends(partial0)
    held[HALO_A_SIB] = after(halo_a_sib, sends0)
    got0 = first_round(sends0)
    partial1 = tiles(1)
    sends1 = first_sends(partial1)
    got0, sends1 = lax.optimization_barrier((got0, sends1))
    got1 = first_round(sends1)
    sends0 = second_sends(partial0, got0)
    more0 = first_round(sends0)
    sends1 = second_sends(partial1, got1)
    far_b, halo_b, minor, more0 = lax.optimization_barrier((far_b, halo_b, minor, more0, sends1))[:4]
    more1 = first_round(sends1)
    held[FAR_B], held[HALO_B], held[MINOR] = far_b, halo_b, minor
    held[FAR_B_SIB] = aux_permute(far_b, [(0, 1, 0), (3, 2, 0)])
    held[HALO_B_SIB] = aux_permute(halo_b, [(2, 3, 0)])
    partial2 = tiles(2)
    sends2 = first_sends(partial2)
    more1 = after(more1, sends2)
    got2 = first_round(sends2)
    total0 = finish(partial0, got0, more0)
    total1 = finish(partial1, got1, more1)
    moved0 = wide(aux_permute(narrow(jnp.concatenate(total1)), [(0, 0, 1)]))
    partial3 = tiles(3)
    sends3 = first_sends(partial3)
    got2 = after(got2, partial3)
    sends2 = second_sends(partial2, got2)
    more2 = first_round(sends2)
    got3 = first_round(after(sends3, sends2))
    more3 = first_round(second_sends(partial3, got3))
    total2 = finish(partial2, got2, more2)
    moved2 = wide(aux_permute(narrow(jnp.concatenate(total2)), [(0, 0, 1), (1, 1, 1), (2, 2, 1)]))
    total3 = finish(partial3, got3, more3)
    slots = jnp.concatenate(total0 + total1 + total2 + total3 + [moved0, moved2])
    parts = pick_parts(entries, slots).reshape(4, 2, 2, PART, ROWS)

    def x_part(k, d):
        return parts[k, d]

    zero, one = ring_sum(x_part, x_permute, narrow, wide)
    final = [zero[0], zero[1], one[0], one[1]]

    swapped = wide(aux_permute(narrow(one[0]), [(2, 3, 0), (3, 2, 0)]))
    lower = [final[0], final[1], jnp.where(x_lo == 1, swapped, final[2]), final[3]]

    crossed = narrow(jnp.stack(final[1:])).reshape(3, PART, 8, PART)
    crossed = lax.all_to_all(crossed, "pair", split_axis=2, concat_axis=1, tiled=True)
    crossed = crossed.reshape(3, ROWS, PART)
    back = [
        [(0, 3, -1), (1, 0, 0), (2, 1, 0), (3, 2, 0)],
        [(0, 2, -1), (1, 3, -1), (2, 1, 0), (3, 0, 0)],
        [(0, 1, -1), (1, 2, -1), (2, 3, -1), (3, 0, 0)],
    ]
    upper = [wide(aux_permute(crossed[o], back[o])).T for o in range(3)]
    return jnp.stack(lower[::-1] + upper)


def solution(mesh):
    return jax.shard_map(
        local,
        mesh=mesh,
        in_specs=(P("aux", "pair"), P("pair"), P("pair"), P(), P()),
        out_specs=P(None, ("aux", "pair"), None),
        check_vma=False,
    )
```

```python
import functools

import jax
import jax.numpy as jnp
import numpy as np
from jax import lax
from jax.experimental import pallas as pl
from jax.experimental.pallas import tpu as pltpu
from jax.sharding import PartitionSpec as P

ROWS = 768
HALF = 3072
PART = 96
PLANES = 4
WIDE = 256
freq_point = 0.5

OWN, SIB, FAR_A, FAR_A_SIB, FAR_B, FAR_B_SIB, HALO_A, HALO_B, HALO_A_SIB, HALO_B_SIB, MINOR = range(11)

WHERE = [
    {"A0": OWN, "A1": SIB, "A2": FAR_B, "A3": FAR_A_SIB, "P0": HALO_A, "B3": MINOR},
    {"A1": OWN, "A0": SIB, "A3": FAR_A, "A2": FAR_B_SIB, "P1": HALO_B},
    {"A2": OWN, "A3": SIB, "A0": FAR_A, "A1": FAR_B_SIB, "B2": HALO_B, "B3": HALO_A_SIB, "P0": MINOR},
    {"A3": OWN, "A2": SIB, "A1": FAR_B, "A0": FAR_A_SIB, "B3": HALO_A, "B2": HALO_B_SIB},
]

BATCHES = [
    [["A0A0", "P0A1"],
     ["A1A0", "A1A1"],
     ["A2A2", "A0A0"],
     ["A3A2", "A3A3"]],
    [["A3A1", "P0A3"],
     ["A3A0", "A3A3"],
     ["A0B3", "A2B3"],
     ["A3A0", "A2A0"]],
    [["P0A2", "A2A1"],
     ["P1A2", "P1A3"],
     ["P0A1", "A0B2"],
     ["A1A0", "A1A1"]],
    [["A2A2", "A2B3"],
     ["A3A2", "A2A0"],
     ["A2A1", "A3A1"],
     ["A1B3", "A1B2"]],
]
MOVED = [["A0B1", "A0B3", "A0B2", None], [None, None, "A1B2", "A1B3"],
         [None, None, "A0B1", None], [None, None, None, None]]
ENTRIES = [
    [["A0A0", "A0B3", "A0B2", "A0B1"], ["A2A2", "A2A1", "A3A1", "A2B3"]],
    [["A1A1", "A1A0", "A1B3", "A1B2"], ["A3A3", "A3A2", "A2A0", "A3A0"]],
]
def batch_tables(batch, sources):
    held_most = 0
    plans = []
    for role, tiles in enumerate(batch):
        held = []
        first = []
        for step, tile in enumerate(tiles):
            for block in (tile[:2], tile[2:]):
                if block not in held:
                    held.append(block)
                    first.append(step)
        plans.append((held, first))
        held_most = max(held_most, len(held))
    rows = []
    for role, tiles in enumerate(batch):
        held, first = plans[role]
        left = [held.index(tile[:2]) for tile in tiles]
        right = [held.index(tile[2:]) for tile in tiles]
        fresh = [int(i == 0 or left[i] != left[i - 1]) for i in range(len(tiles))]
        pad = held_most - len(held)
        source = [sources.index(WHERE[role][block]) for block in held] + [-1] * pad
        rows.append(left + right + fresh + source + first + [-1] * pad)
    return np.array(rows, np.int32), held_most


def tiles_kernel(count, held_most, sources, table, weight, *refs):
    source_refs = refs[:sources]
    out, held, scaled, sems = refs[sources:]
    step = pl.program_id(0)
    source_at = 3 * count
    first_at = source_at + held_most

    @pl.when(step == 0)
    def _():
        for j in range(held_most):
            for k in range(sources):
                @pl.when(table[source_at + j] == k)
                def _():
                    pltpu.make_async_copy(source_refs[k], held.at[j], sems.at[j]).start()

    def wait(block):
        for j in range(held_most):
            @pl.when((table[first_at + j] == step) & (block == j))
            def _():
                pltpu.make_async_copy(source_refs[0], held.at[j], sems.at[j]).wait()

    left = table[step]
    right = table[count + step]
    wait(left)

    @pl.when(table[2 * count + step] == 1)
    def _():
        @pl.loop(0, ROWS // 32)
        def _(i):
            rows = pl.ds(pl.multiple_of(i * 32, 32), 32)
            scaled[rows, :] = (held[left, rows, :].astype(jnp.float32) * weight[...]).astype(jnp.bfloat16)

    @pl.when(left != right)
    def _():
        wait(right)

    here = table[first_at + held_most]
    for n in range(ROWS // WIDE):
        columns = slice(n * WIDE, (n + 1) * WIDE)
        acc = lax.dot_general(
            scaled[...], held[right, columns, :],
            (((1,), (1,)), ((), ())), preferred_element_type=jnp.float32)
        for y in range(4):
            at = lax.rem(y + 4 - here, 4)
            for h in range(2):
                first = (h * 4 + y) * PART
                out[at, h, 0, :, columns] = acc[first:first + PART]


def tile_batch(batch, table_row, held_most, weight, sources):
    count = len(batch[0])
    return pl.pallas_call(
        functools.partial(tiles_kernel, count, held_most, len(sources)),
        grid_spec=pltpu.PrefetchScalarGridSpec(
            num_scalar_prefetch=1,
            grid=(count,),
            in_specs=[pl.BlockSpec((1, HALF), lambda i, t: (0, 0))]
            + [pl.BlockSpec(memory_space=pl.ANY)] * len(sources),
            out_specs=pl.BlockSpec((4, 2, 1, PART, ROWS), lambda i, t: (0, 0, i, 0, 0)),
            scratch_shapes=[
                pltpu.VMEM((held_most, ROWS, HALF), jnp.bfloat16),
                pltpu.VMEM((ROWS, HALF), jnp.bfloat16),
                pltpu.SemaphoreType.DMA((held_most,)),
            ],
        ),
        out_shape=jax.ShapeDtypeStruct((4, 2, count, PART, ROWS), jnp.float32),
        compiler_params=pltpu.CompilerParams(
            dimension_semantics=("arbitrary",), vmem_limit_bytes=56 * 1024 * 1024),
        cost_estimate=pl.CostEstimate(
            flops=count * ROWS * ROWS,
            bytes_accessed=count * ROWS * ROWS,
            transcendentals=0),
    )(table_row, weight, *sources)


def lookup(table, index):
    blocks = table.shape[0]
    high = lax.shift_right_logical(index, 7)
    low = jnp.bitwise_and(index, 127)
    pairs = index.shape[1]
    hot = jnp.where(lax.broadcasted_iota(jnp.int32, (blocks, pairs), 0) == high, 1.0, 0.0).astype(jnp.bfloat16)
    rest = table
    column = jnp.zeros((128, pairs), jnp.float32)
    for _ in range(3):
        piece = rest.astype(jnp.bfloat16)
        rest = rest - piece.astype(jnp.float32)
        column = column + lax.dot_general(
            piece, hot, (((0,), (0,)), ((), ())), preferred_element_type=jnp.float32)
    mask = lax.broadcasted_iota(jnp.int32, (128, pairs), 0) == low
    return jnp.sum(jnp.where(mask, column, 0.0), axis=0, keepdims=True)


def gap_kernel(occ_index, virt_index, occ_energy, virt_energy, gap):
    gap[...] = lookup(virt_energy[...], virt_index[...]) - lookup(occ_energy[...], occ_index[...])


def pair_gaps(occ_index, virt_index, occ_energy, virt_energy):
    block = 512
    pairs = occ_index.shape[0]
    occ_table = occ_energy.reshape(-1, 128)
    virt_table = virt_energy.reshape(-1, 128)
    line = pl.BlockSpec((1, block), lambda i: (0, i))
    return pl.pallas_call(
        gap_kernel,
        grid=(pairs // block,),
        in_specs=[line, line,
                  pl.BlockSpec(occ_table.shape, lambda i: (0, 0)),
                  pl.BlockSpec(virt_table.shape, lambda i: (0, 0))],
        out_specs=line,
        out_shape=jax.ShapeDtypeStruct((1, pairs), jnp.float32),
        cost_estimate=pl.CostEstimate(flops=6 * 128 * 288 * pairs, bytes_accessed=200000, transcendentals=0),
    )(occ_index[None, :], virt_index[None, :], occ_table, virt_table)


def halves_kernel(x_lo, coeffs, mine, other, largest):
    for low in range(2):
        @pl.when(x_lo[0] == low)
        def _():
            mine[...] = coeffs[:, low * HALF:(low + 1) * HALF]
            other[...] = coeffs[:, (1 - low) * HALF:(2 - low) * HALF]

    @pl.when(pl.program_id(0) == 0)
    def _():
        largest[...] = jnp.zeros_like(largest)

    top = jnp.zeros((coeffs.shape[0], 128), jnp.float32)
    for c in range(coeffs.shape[1] // 128):
        top = jnp.maximum(top, jnp.abs(coeffs[:, c * 128:(c + 1) * 128].astype(jnp.float32)))
    largest[...] = jnp.maximum(largest[...], jnp.max(top.reshape(-1, 8, 128), axis=0))


def cut_in_halves(x_lo, coeffs):
    half = jax.ShapeDtypeStruct((ROWS, HALF), jnp.bfloat16)
    block = pl.BlockSpec((PART, HALF), lambda i, t: (i, 0))
    return pl.pallas_call(
        halves_kernel,
        grid_spec=pltpu.PrefetchScalarGridSpec(
            num_scalar_prefetch=1,
            grid=(ROWS // PART,),
            in_specs=[pl.BlockSpec((PART, 2 * HALF), lambda i, t: (i, 0))],
            out_specs=[block, block, pl.BlockSpec((8, 128), lambda i, t: (0, 0))],
        ),
        out_shape=[half, half, jax.ShapeDtypeStruct((8, 128), jnp.float32)],
        compiler_params=pltpu.CompilerParams(vmem_limit_bytes=24 * 1024 * 1024),
        cost_estimate=pl.CostEstimate(flops=0, bytes_accessed=PART * ROWS, transcendentals=0),
    )(x_lo[None], coeffs)


def moves(pairs):
    return [(z * 4 + src, (z + dz) % PLANES * 4 + dst) for z in range(PLANES) for src, dst, dz in pairs]


def aux_permute(value, pairs):
    return lax.ppermute(value, "aux", moves(pairs))


def y_permute(value, by):
    return lax.ppermute(value, "pair", [(h * 4 + y, h * 4 + (y + by) % 4) for h in range(2) for y in range(4)])


def x_permute(value, by):
    perm = []
    for z in range(PLANES):
        for x in range(4):
            to = (x + by) % 4
            for core in range(2):
                for y in range(4):
                    source = (z * 4 + x % 2 * 2 + core) * 8 + x // 2 * 4 + y
                    perm.append((source, (z * 4 + to % 2 * 2 + core) * 8 + to // 2 * 4 + y))
    return lax.ppermute(value, ("aux", "pair"), perm)


def both_ways(permute, up, down):
    return lax.optimization_barrier((permute(up, 1), permute(down, -1)))


def ring_sum(part, permute, scales):
    count = part(0, 0).shape[0]
    up, down = both_ways(permute, narrow(jnp.concatenate([part(2, 0), part(1, 1)]), scales),
                         narrow(jnp.concatenate([part(2, 1), part(3, 0)]), scales))
    up_more, down_more = both_ways(permute, narrow(part(1, 0) + wide(up[:count], scales), scales),
                                   narrow(part(3, 1) + wide(down[:count], scales), scales))
    zero = part(0, 0) + wide(down[count:], scales) + wide(up_more, scales)
    one = part(0, 1) + wide(up[count:], scales) + wide(down_more, scales)
    return zero, one


def slot_names(role):
    names = []
    for batch in BATCHES:
        names += [(tile, h) for h in range(2) for tile in batch[role]]
    early, late = MOVED[role][:2], MOVED[role][2:]
    names += [(tile, h) for h in range(2) for tile in early]
    names += [(tile, h) for h in range(2) for tile in late]
    return names


def entry_table():
    rows = []
    for role in range(4):
        names = slot_names(role)
        for x_hi in range(2):
            row = []
            for k in range(4):
                to = (x_hi * 2 + role // 2 + k) % 4
                row += [names.index((tile, to // 2)) for tile in ENTRIES[role % 2][to % 2]]
            rows.append(row)
    return np.array(rows, np.int32)


def pick_kernel(table, slots, parts):
    for i in range(16):
        parts[i] = slots[table[i]]


def pick_parts(table, slots):
    return pl.pallas_call(
        pick_kernel,
        in_specs=[pl.BlockSpec(memory_space=pltpu.SMEM), pl.BlockSpec(memory_space=pltpu.VMEM)],
        out_specs=pl.BlockSpec(memory_space=pltpu.VMEM),
        out_shape=jax.ShapeDtypeStruct((16, PART, ROWS), jnp.float32),
        compiler_params=pltpu.CompilerParams(vmem_limit_bytes=20 * 1024 * 1024),
        cost_estimate=pl.CostEstimate(flops=0, bytes_accessed=PART * ROWS, transcendentals=0),
    )(table, slots)


def largest_round(value, permute):
    got = [permute(value, by) for by in (1, 2, 3)]
    return jnp.maximum(jnp.maximum(value, got[0]), jnp.maximum(got[1], got[2]))


def z_permute(value, by):
    return aux_permute(value, [(r, r, by) for r in range(4)])


def scales_of(largest):
    bound = 8.0 * HALF * 4 * largest * largest * 4.0
    scale = 32768.0 / jnp.maximum(bound, 1e-30)
    return scale, 1.0 / scale


def narrow(value, scales):
    return (value * scales[0]).astype(jnp.float16)


def wide(value, scales):
    return value.astype(jnp.float32) * scales[1]


def after(value, other):
    return lax.optimization_barrier((value, other))[0]


def local(coeffs, occ_index, virt_index, occ_energy, virt_energy):
    role = lax.rem(lax.axis_index("aux"), 4)
    x_lo = role // 2
    x_hi = lax.axis_index("pair") // 4
    y = lax.rem(lax.axis_index("pair"), 4)

    mine, other, largest = cut_in_halves(x_lo.astype(jnp.int32), coeffs)
    side = [(0, 2, 0), (1, 3, 0), (2, 0, 0), (3, 1, 0)]
    near = [aux_permute(largest, side), z_permute(largest, 1), z_permute(largest, -1)]
    mine, other, near = lax.optimization_barrier((mine, other, near))
    halo_a = aux_permute(mine, [(0, 0, -1), (3, 3, 1)])
    far_a = aux_permute(other, [(0, 2, 0), (3, 1, 0)])
    sib = aux_permute(mine, [(0, 1, 0), (1, 0, 0), (2, 3, 0), (3, 2, 0)])

    largest = jnp.maximum(jnp.maximum(largest, near[0]), jnp.maximum(near[1], near[2]))
    largest = jnp.maximum(largest, aux_permute(largest, [(0, 1, 0), (1, 0, 0), (2, 3, 0), (3, 2, 0)]))
    largest = largest_round(largest, y_permute)
    early = scales_of(jnp.max(largest))

    occ_index, virt_index = after([occ_index, virt_index], mine)
    begin = x_lo * HALF
    gap = pair_gaps(
        lax.dynamic_slice_in_dim(occ_index, begin, HALF),
        lax.dynamic_slice_in_dim(virt_index, begin, HALF),
        occ_energy, virt_energy)
    weight = -4.0 * gap / (gap * gap + freq_point * freq_point)

    plans = []
    for batch in BATCHES:
        used = sorted({WHERE[r][t[i:i + 2]] for r in range(4) for t in batch[r] for i in (0, 2)})
        table, held_most = batch_tables(batch, used)
        row = lax.dynamic_index_in_dim(jnp.asarray(table), role, axis=0, keepdims=False)
        row = jnp.concatenate([row, y[None].astype(jnp.int32)])
        plans.append([used, row, held_most])
    entries = lax.dynamic_index_in_dim(jnp.asarray(entry_table()), role * 2 + x_hi, axis=0, keepdims=False)
    rows = [plan[1] for plan in plans]
    far_a, halo_a, sib, early, largest, weight, entries, rows = lax.optimization_barrier(
        (far_a, halo_a, sib, early, largest, weight, entries, rows))

    far_b = aux_permute(after(other, far_a), [(1, 3, 0), (2, 0, 0)])
    halo_b = aux_permute(after(mine, halo_a), [(1, 1, -1), (2, 2, 1)])
    far_a_sib = aux_permute(far_a, [(1, 0, 0), (2, 3, 0)])
    halo_a_sib = aux_permute(halo_a, [(3, 2, 0)])
    minor = aux_permute(far_a, [(1, 0, 1), (2, 2, -1)])

    held = {OWN: mine, SIB: sib, FAR_A: far_a, HALO_A: halo_a}

    def tiles(number):
        used, _, held_most = plans[number]
        return tile_batch(BATCHES[number], rows[number], held_most, weight, [held[s] for s in used])

    def first_sends(partial, scales):
        return [narrow(jnp.concatenate([partial[2, 0], partial[1, 1]]), scales),
                narrow(jnp.concatenate([partial[2, 1], partial[3, 0]]), scales)]

    def first_round(sends):
        return [y_permute(sends[0], 1), y_permute(sends[1], -1)]

    def second_sends(partial, got, scales):
        return [narrow(partial[1, 0] + wide(got[0][:2], scales), scales),
                narrow(partial[3, 1] + wide(got[1][:2], scales), scales)]

    def finish(partial, got, more, scales):
        zero = partial[0, 0] + wide(got[1][2:], scales) + wide(more[0], scales)
        one = partial[0, 1] + wide(got[0][2:], scales) + wide(more[1], scales)
        return [zero, one]

    partial0 = tiles(0)
    sends0 = first_sends(partial0, early)
    held[FAR_A_SIB], held[HALO_A_SIB] = after([far_a_sib, halo_a_sib], sends0)
    got0 = first_round(sends0)
    partial1 = tiles(1)
    sends1 = first_sends(partial1, early)
    got0, sends1 = lax.optimization_barrier((got0, sends1))
    got1 = first_round(sends1)
    sends0 = second_sends(partial0, got0, early)
    more0 = first_round(sends0)
    far_b, halo_b, minor, got1, largest = lax.optimization_barrier(
        (far_b, halo_b, minor, got1, largest, sends0))[:5]
    more1 = first_round(second_sends(partial1, got1, early))
    held[FAR_B], held[HALO_B], held[MINOR] = far_b, halo_b, minor
    held[FAR_B_SIB] = aux_permute(far_b, [(0, 1, 0), (3, 2, 0)])
    held[HALO_B_SIB] = aux_permute(halo_b, [(2, 3, 0)])
    largest = jnp.maximum(largest, x_permute(largest, 2))
    largest = jnp.maximum(largest, z_permute(largest, 2))
    largest = jnp.maximum(largest, aux_permute(largest, side))
    late = scales_of(jnp.max(largest))
    partial2 = tiles(2)
    sends2 = first_sends(partial2, late)
    more0, more1 = after([more0, more1], sends2)
    got2 = first_round(sends2)
    rows[3], more0 = lax.optimization_barrier((rows[3], more0, sends2))[:2]
    partial3 = tiles(3)
    total0 = finish(partial0, got0, more0, early)
    total1 = finish(partial1, got1, more1, early)
    moved0 = jnp.stack([total0[0][1], total1[0][1], total0[1][1], total1[1][1]])
    moved0 = wide(aux_permute(narrow(moved0, late), [(0, 0, 1)]), late)
    sends3 = first_sends(partial3, late)
    got2 = after(got2, partial3)
    sends2 = second_sends(partial2, got2, late)
    more2 = first_round(sends2)
    sends3 = after(sends3, sends2)
    got3 = first_round(sends3)
    more2 = after(more2, sends3)
    total2 = finish(partial2, got2, more2, late)
    moved2 = aux_permute(narrow(jnp.concatenate(total2), late), [(0, 0, 1), (1, 1, 1), (2, 2, 1)])
    moved2 = wide(moved2, late)
    more3 = both_ways(y_permute, *second_sends(partial3, got3, late))
    total3 = finish(partial3, got3, more3, late)
    slots = jnp.concatenate(total0 + total1 + total2 + total3 + [moved0, moved2])
    parts = pick_parts(entries, slots).reshape(4, 2, 2, PART, ROWS)

    def x_part(k, d):
        return parts[k, d]

    zero, one = ring_sum(x_part, x_permute, late)
    final = [zero[0], zero[1], one[0], one[1]]

    crossed = narrow(jnp.stack(final[1:]), late).reshape(3, PART, 8, PART)
    crossed = lax.all_to_all(crossed, "pair", split_axis=2, concat_axis=1, tiled=True)
    crossed = crossed.reshape(3, ROWS, PART)

    swapped = aux_permute(after(narrow(one[0], late), crossed), [(2, 3, 0), (3, 2, 0)])
    lower = [final[0], final[1], jnp.where(x_lo == 1, wide(swapped, late), final[2]), final[3]]

    back = [
        [(0, 3, -1), (1, 0, 0), (2, 1, 0), (3, 2, 0)],
        [(0, 2, -1), (1, 3, -1), (2, 1, 0), (3, 0, 0)],
        [(0, 1, -1), (1, 2, -1), (2, 3, -1), (3, 0, 0)],
    ]
    upper = [wide(aux_permute(crossed[o], back[o]), late).T for o in range(3)]
    return jnp.stack(lower[::-1] + upper)


def solution(mesh):
    return jax.shard_map(
        local,
        mesh=mesh,
        in_specs=(P("aux", "pair"), P("pair"), P("pair"), P(), P()),
        out_specs=P(None, ("aux", "pair"), None),
        check_vma=False,
    )
```

```python
import functools

import jax
import jax.numpy as jnp
import numpy as np
from jax import lax
from jax.experimental import pallas as pl
from jax.experimental.pallas import tpu as pltpu
from jax.sharding import PartitionSpec as P

ROWS = 768
HALF = 3072
PART = 96
PLANES = 4
WIDE = 256
freq_point = 0.5

OWN, SIB, FAR_A, FAR_A_SIB, FAR_B, FAR_B_SIB, HALO_A, HALO_B, HALO_A_SIB, HALO_B_SIB, MINOR = range(11)

WHERE = [
    {"A0": OWN, "A1": SIB, "A2": FAR_B, "A3": FAR_A_SIB, "P0": HALO_A, "B3": MINOR},
    {"A1": OWN, "A0": SIB, "A3": FAR_A, "A2": FAR_B_SIB, "P1": HALO_B},
    {"A2": OWN, "A3": SIB, "A0": FAR_A, "A1": FAR_B_SIB, "B2": HALO_B, "B3": HALO_A_SIB, "P0": MINOR},
    {"A3": OWN, "A2": SIB, "A1": FAR_B, "A0": FAR_A_SIB, "B3": HALO_A, "B2": HALO_B_SIB},
]

BATCHES = [
    [["A0A0", "P0A1"],
     ["A1A0", "A1A1"],
     ["A2A2", "A0A0"],
     ["A3A2", "A3A3"]],
    [["A3A1", "P0A3"],
     ["A3A0", "A3A3"],
     ["A0B3", "A2B3"],
     ["A3A0", "A2A0"]],
    [["P0A2", "A2A1"],
     ["P1A2", "P1A3"],
     ["P0A1", "A0B2"],
     ["A1A0", "A1A1"]],
    [["A2A2", "A2B3"],
     ["A3A2", "A2A0"],
     ["A2A1", "A3A1"],
     ["A1B3", "A1B2"]],
]
MOVED = [["A0B1", "A0B3", "A0B2", None], [None, None, "A1B2", "A1B3"],
         [None, None, "A0B1", None], [None, None, None, None]]
ENTRIES = [
    [["A0A0", "A0B3", "A0B2", "A0B1"], ["A2A2", "A2A1", "A3A1", "A2B3"]],
    [["A1A1", "A1A0", "A1B3", "A1B2"], ["A3A3", "A3A2", "A2A0", "A3A0"]],
]
def batch_tables(batch, sources):
    held_most = 0
    plans = []
    for role, tiles in enumerate(batch):
        held = []
        first = []
        for step, tile in enumerate(tiles):
            for block in (tile[:2], tile[2:]):
                if block not in held:
                    held.append(block)
                    first.append(step)
        plans.append((held, first))
        held_most = max(held_most, len(held))
    rows = []
    for role, tiles in enumerate(batch):
        held, first = plans[role]
        left = [held.index(tile[:2]) for tile in tiles]
        right = [held.index(tile[2:]) for tile in tiles]
        fresh = [int(i == 0 or left[i] != left[i - 1]) for i in range(len(tiles))]
        pad = held_most - len(held)
        source = [sources.index(WHERE[role][block]) for block in held] + [-1] * pad
        rows.append(left + right + fresh + source + first + [-1] * pad)
    return np.array(rows, np.int32), held_most


def tiles_kernel(count, held_most, sources, table, weight, *refs):
    source_refs = refs[:sources]
    out, held, scaled, sems = refs[sources:]
    step = pl.program_id(0)
    source_at = 3 * count
    first_at = source_at + held_most

    @pl.when(step == 0)
    def _():
        for j in range(held_most):
            for k in range(sources):
                @pl.when(table[source_at + j] == k)
                def _():
                    pltpu.make_async_copy(source_refs[k], held.at[j], sems.at[j]).start()

    def wait(block):
        for j in range(held_most):
            @pl.when((table[first_at + j] == step) & (block == j))
            def _():
                pltpu.make_async_copy(source_refs[0], held.at[j], sems.at[j]).wait()

    left = table[step]
    right = table[count + step]
    wait(left)

    @pl.when(table[2 * count + step] == 1)
    def _():
        @pl.loop(0, ROWS // 32)
        def _(i):
            rows = pl.ds(pl.multiple_of(i * 32, 32), 32)
            scaled[rows, :] = (held[left, rows, :].astype(jnp.float32) * weight[...]).astype(jnp.bfloat16)

    @pl.when(left != right)
    def _():
        wait(right)

    here = table[first_at + held_most]
    for n in range(ROWS // WIDE):
        columns = slice(n * WIDE, (n + 1) * WIDE)
        acc = lax.dot_general(
            scaled[...], held[right, columns, :],
            (((1,), (1,)), ((), ())), preferred_element_type=jnp.float32)
        for y in range(4):
            at = lax.rem(y + 4 - here, 4)
            for h in range(2):
                first = (h * 4 + y) * PART
                out[at, h, 0, :, columns] = acc[first:first + PART]


def tile_batch(batch, table_row, held_most, weight, sources):
    count = len(batch[0])
    return pl.pallas_call(
        functools.partial(tiles_kernel, count, held_most, len(sources)),
        grid_spec=pltpu.PrefetchScalarGridSpec(
            num_scalar_prefetch=1,
            grid=(count,),
            in_specs=[pl.BlockSpec((1, HALF), lambda i, t: (0, 0))]
            + [pl.BlockSpec(memory_space=pl.ANY)] * len(sources),
            out_specs=pl.BlockSpec((4, 2, 1, PART, ROWS), lambda i, t: (0, 0, i, 0, 0)),
            scratch_shapes=[
                pltpu.VMEM((held_most, ROWS, HALF), jnp.bfloat16),
                pltpu.VMEM((ROWS, HALF), jnp.bfloat16),
                pltpu.SemaphoreType.DMA((held_most,)),
            ],
        ),
        out_shape=jax.ShapeDtypeStruct((4, 2, count, PART, ROWS), jnp.float32),
        compiler_params=pltpu.CompilerParams(
            dimension_semantics=("arbitrary",), vmem_limit_bytes=56 * 1024 * 1024),
        cost_estimate=pl.CostEstimate(
            flops=count * ROWS * ROWS,
            bytes_accessed=count * ROWS * ROWS,
            transcendentals=0),
    )(table_row, weight, *sources)


def lookup(table, index):
    blocks = table.shape[0]
    high = lax.shift_right_logical(index, 7)
    low = jnp.bitwise_and(index, 127)
    pairs = index.shape[1]
    hot = jnp.where(lax.broadcasted_iota(jnp.int32, (blocks, pairs), 0) == high, 1.0, 0.0).astype(jnp.bfloat16)
    rest = table
    column = jnp.zeros((128, pairs), jnp.float32)
    for _ in range(3):
        piece = rest.astype(jnp.bfloat16)
        rest = rest - piece.astype(jnp.float32)
        column = column + lax.dot_general(
            piece, hot, (((0,), (0,)), ((), ())), preferred_element_type=jnp.float32)
    mask = lax.broadcasted_iota(jnp.int32, (128, pairs), 0) == low
    return jnp.sum(jnp.where(mask, column, 0.0), axis=0, keepdims=True)


def gap_kernel(occ_index, virt_index, occ_energy, virt_energy, gap):
    gap[...] = lookup(virt_energy[...], virt_index[...]) - lookup(occ_energy[...], occ_index[...])


def pair_gaps(occ_index, virt_index, occ_energy, virt_energy):
    block = 512
    pairs = occ_index.shape[0]
    occ_table = occ_energy.reshape(-1, 128)
    virt_table = virt_energy.reshape(-1, 128)
    line = pl.BlockSpec((1, block), lambda i: (0, i))
    return pl.pallas_call(
        gap_kernel,
        grid=(pairs // block,),
        in_specs=[line, line,
                  pl.BlockSpec(occ_table.shape, lambda i: (0, 0)),
                  pl.BlockSpec(virt_table.shape, lambda i: (0, 0))],
        out_specs=line,
        out_shape=jax.ShapeDtypeStruct((1, pairs), jnp.float32),
        cost_estimate=pl.CostEstimate(flops=6 * 128 * 288 * pairs, bytes_accessed=200000, transcendentals=0),
    )(occ_index[None, :], virt_index[None, :], occ_table, virt_table)


def halves_kernel(x_lo, coeffs, mine, other, largest):
    for low in range(2):
        @pl.when(x_lo[0] == low)
        def _():
            mine[...] = coeffs[:, low * HALF:(low + 1) * HALF]
            other[...] = coeffs[:, (1 - low) * HALF:(2 - low) * HALF]

    @pl.when(pl.program_id(0) == 0)
    def _():
        largest[...] = jnp.zeros_like(largest)

    top = jnp.zeros((coeffs.shape[0], 128), jnp.float32)
    for c in range(coeffs.shape[1] // 128):
        top = jnp.maximum(top, jnp.abs(coeffs[:, c * 128:(c + 1) * 128].astype(jnp.float32)))
    largest[...] = jnp.maximum(largest[...], jnp.max(top.reshape(-1, 8, 128), axis=0))


def cut_in_halves(x_lo, coeffs):
    half = jax.ShapeDtypeStruct((ROWS, HALF), jnp.bfloat16)
    block = pl.BlockSpec((PART, HALF), lambda i, t: (i, 0))
    return pl.pallas_call(
        halves_kernel,
        grid_spec=pltpu.PrefetchScalarGridSpec(
            num_scalar_prefetch=1,
            grid=(ROWS // PART,),
            in_specs=[pl.BlockSpec((PART, 2 * HALF), lambda i, t: (i, 0))],
            out_specs=[block, block, pl.BlockSpec((8, 128), lambda i, t: (0, 0))],
        ),
        out_shape=[half, half, jax.ShapeDtypeStruct((8, 128), jnp.float32)],
        compiler_params=pltpu.CompilerParams(vmem_limit_bytes=24 * 1024 * 1024),
        cost_estimate=pl.CostEstimate(flops=0, bytes_accessed=PART * ROWS, transcendentals=0),
    )(x_lo[None], coeffs)


def moves(pairs):
    return [(z * 4 + src, (z + dz) % PLANES * 4 + dst) for z in range(PLANES) for src, dst, dz in pairs]


def aux_permute(value, pairs):
    return lax.ppermute(value, "aux", moves(pairs))


def y_permute(value, by):
    return lax.ppermute(value, "pair", [(h * 4 + y, h * 4 + (y + by) % 4) for h in range(2) for y in range(4)])


def x_permute(value, by, roles=range(4)):
    perm = []
    for z in range(PLANES):
        for x in range(4):
            to = (x + by) % 4
            for core in range(2):
                if x % 2 * 2 + core not in roles:
                    continue
                for y in range(4):
                    source = (z * 4 + x % 2 * 2 + core) * 8 + x // 2 * 4 + y
                    perm.append((source, (z * 4 + to % 2 * 2 + core) * 8 + to // 2 * 4 + y))
    return lax.ppermute(value, ("aux", "pair"), perm)


def both_ways(permute, up, down):
    return lax.optimization_barrier((permute(up, 1), permute(down, -1)))


def ring_sum(part, permute, scales):
    count = part(0, 0).shape[0]
    up, down = both_ways(permute, narrow(jnp.concatenate([part(2, 0), part(1, 1)]), scales),
                         narrow(jnp.concatenate([part(2, 1), part(3, 0)]), scales))
    up_more, down_more = both_ways(permute, narrow(part(1, 0) + wide(up[:count], scales), scales),
                                   narrow(part(3, 1) + wide(down[:count], scales), scales))
    zero = part(0, 0) + wide(down[count:], scales) + wide(up_more, scales)
    one = part(0, 1) + wide(up[count:], scales) + wide(down_more, scales)
    return zero, one


def slot_names(role):
    names = []
    for batch in BATCHES:
        names += [(tile, h) for h in range(2) for tile in batch[role]]
    early, late = MOVED[role][:2], MOVED[role][2:]
    names += [(tile, h) for h in range(2) for tile in early]
    names += [(tile, h) for h in range(2) for tile in late]
    return names


def entry_table():
    rows = []
    for role in range(4):
        names = slot_names(role)
        for x_hi in range(2):
            row = []
            for k in range(4):
                to = (x_hi * 2 + role // 2 + k) % 4
                row += [names.index((tile, to // 2)) for tile in ENTRIES[role % 2][to % 2]]
            rows.append(row)
    return np.array(rows, np.int32)


def pick_kernel(table, slots, parts):
    for i in range(16):
        parts[i] = slots[table[i]]


def pick_parts(table, slots):
    return pl.pallas_call(
        pick_kernel,
        in_specs=[pl.BlockSpec(memory_space=pltpu.SMEM), pl.BlockSpec(memory_space=pltpu.VMEM)],
        out_specs=pl.BlockSpec(memory_space=pltpu.VMEM),
        out_shape=jax.ShapeDtypeStruct((16, PART, ROWS), jnp.float32),
        compiler_params=pltpu.CompilerParams(vmem_limit_bytes=20 * 1024 * 1024),
        cost_estimate=pl.CostEstimate(flops=0, bytes_accessed=PART * ROWS, transcendentals=0),
    )(table, slots)


def largest_round(value, permute):
    got = [permute(value, by) for by in (1, 2, 3)]
    return jnp.maximum(jnp.maximum(value, got[0]), jnp.maximum(got[1], got[2]))


def scales_of(largest):
    bound = 8.0 * HALF * 4 * largest * largest * 4.0
    scale = 32768.0 / jnp.maximum(bound, 1e-30)
    return scale, 1.0 / scale


def narrow(value, scales):
    return (value * scales[0]).astype(jnp.float16)


def wide(value, scales):
    return value.astype(jnp.float32) * scales[1]


def after(value, other):
    return lax.optimization_barrier((value, other))[0]


def local(coeffs, occ_index, virt_index, occ_energy, virt_energy):
    role = lax.rem(lax.axis_index("aux"), 4)
    x_lo = role // 2
    x_hi = lax.axis_index("pair") // 4
    y = lax.rem(lax.axis_index("pair"), 4)

    mine, other, largest = cut_in_halves(x_lo.astype(jnp.int32), coeffs)
    halo_a = aux_permute(mine, [(0, 0, -1), (3, 3, 1)])
    far_a = aux_permute(other, [(0, 2, 0), (3, 1, 0)])
    sib = aux_permute(mine, [(0, 1, 0), (1, 0, 0), (2, 3, 0), (3, 2, 0)])

    largest = jnp.maximum(largest, aux_permute(largest, [(0, 1, 0), (1, 0, 0), (2, 3, 0), (3, 2, 0)]))
    largest = largest_round(largest, y_permute)
    largest = jnp.maximum(largest, x_permute(largest, 2, (1, 2)))
    largest = jnp.maximum(largest, aux_permute(largest, [(1, 2, 0), (2, 1, 0)]))
    largest = jnp.maximum(largest, aux_permute(largest, [(1, 1, 2), (2, 2, 2)]))
    largest = jnp.maximum(largest, aux_permute(largest, [(1, 1, 1), (2, 2, 1)]))
    largest = jnp.maximum(largest, aux_permute(largest, [(1, 0, 0), (2, 3, 0)]))
    scales = scales_of(jnp.max(largest))

    occ_index, virt_index = after([occ_index, virt_index], mine)
    begin = x_lo * HALF
    gap = pair_gaps(
        lax.dynamic_slice_in_dim(occ_index, begin, HALF),
        lax.dynamic_slice_in_dim(virt_index, begin, HALF),
        occ_energy, virt_energy)
    weight = -4.0 * gap / (gap * gap + freq_point * freq_point)

    plans = []
    for batch in BATCHES:
        used = sorted({WHERE[r][t[i:i + 2]] for r in range(4) for t in batch[r] for i in (0, 2)})
        table, held_most = batch_tables(batch, used)
        row = lax.dynamic_index_in_dim(jnp.asarray(table), role, axis=0, keepdims=False)
        row = jnp.concatenate([row, y[None].astype(jnp.int32)])
        plans.append([used, row, held_most])
    entries = lax.dynamic_index_in_dim(jnp.asarray(entry_table()), role * 2 + x_hi, axis=0, keepdims=False)
    rows = [plan[1] for plan in plans]
    far_a, halo_a, sib, scales, weight, entries, rows = lax.optimization_barrier(
        (far_a, halo_a, sib, scales, weight, entries, rows))

    far_b = aux_permute(after(other, far_a), [(1, 3, 0), (2, 0, 0)])
    halo_b = aux_permute(after(mine, halo_a), [(1, 1, -1), (2, 2, 1)])
    far_a_sib = aux_permute(far_a, [(1, 0, 0), (2, 3, 0)])
    halo_a_sib = aux_permute(halo_a, [(3, 2, 0)])
    minor = aux_permute(far_a, [(1, 0, 1), (2, 2, -1)])

    held = {OWN: mine, SIB: sib, FAR_A: far_a, HALO_A: halo_a}

    def tiles(number):
        used, _, held_most = plans[number]
        return tile_batch(BATCHES[number], rows[number], held_most, weight, [held[s] for s in used])

    def first_sends(partial, scales):
        return [narrow(jnp.concatenate([partial[2, 0], partial[1, 1]]), scales),
                narrow(jnp.concatenate([partial[2, 1], partial[3, 0]]), scales)]

    def first_round(sends):
        return [y_permute(sends[0], 1), y_permute(sends[1], -1)]

    def second_sends(partial, got, scales):
        return [narrow(partial[1, 0] + wide(got[0][:2], scales), scales),
                narrow(partial[3, 1] + wide(got[1][:2], scales), scales)]

    def finish(partial, got, more, scales):
        zero = partial[0, 0] + wide(got[1][2:], scales) + wide(more[0], scales)
        one = partial[0, 1] + wide(got[0][2:], scales) + wide(more[1], scales)
        return [zero, one]

    partial0 = tiles(0)
    sends0 = first_sends(partial0, scales)
    held[FAR_A_SIB], held[HALO_A_SIB] = after([far_a_sib, halo_a_sib], sends0)
    got0 = first_round(sends0)
    partial1 = tiles(1)
    sends1 = first_sends(partial1, scales)
    got0, sends1 = lax.optimization_barrier((got0, sends1))
    got1 = first_round(sends1)
    sends0 = second_sends(partial0, got0, scales)
    more0 = first_round(sends0)
    far_b, halo_b, minor, got1 = lax.optimization_barrier((far_b, halo_b, minor, got1, sends0))[:4]
    more1 = first_round(second_sends(partial1, got1, scales))
    held[FAR_B], held[HALO_B], held[MINOR] = far_b, halo_b, minor
    held[FAR_B_SIB] = aux_permute(far_b, [(0, 1, 0), (3, 2, 0)])
    held[HALO_B_SIB] = aux_permute(halo_b, [(2, 3, 0)])
    partial2 = tiles(2)
    sends2 = first_sends(partial2, scales)
    got2 = first_round(sends2)
    rows[3], more0 = lax.optimization_barrier((rows[3], more0, sends2))[:2]
    partial3 = tiles(3)
    more0, more1 = after([more0, more1], partial3)
    total0 = finish(partial0, got0, more0, scales)
    total1 = finish(partial1, got1, more1, scales)
    moved0 = jnp.stack([total0[0][1], total1[0][1], total0[1][1], total1[1][1]])
    moved0 = aux_permute(narrow(moved0, scales), [(0, 0, 1)])
    sends3 = first_sends(partial3, scales)
    got2 = after(got2, partial3)
    sends2 = second_sends(partial2, got2, scales)
    more2 = first_round(sends2)
    sends3 = after(sends3, sends2)
    got3 = first_round(sends3)
    more2 = after(more2, sends3)
    total2 = finish(partial2, got2, more2, scales)
    moved2 = narrow(jnp.concatenate(total2), scales)
    moved2 = aux_permute(moved2, [(0, 0, 1), (1, 1, 1), (2, 2, 1)])
    got3, moved2, moved0 = lax.optimization_barrier((got3, moved2, moved0))
    more3 = both_ways(y_permute, *second_sends(partial3, got3, scales))
    moved0, moved2 = wide(moved0, scales), wide(moved2, scales)
    total3 = finish(partial3, got3, more3, scales)
    slots = jnp.concatenate(total0 + total1 + total2 + total3 + [moved0, moved2])
    parts = pick_parts(entries, slots).reshape(4, 2, 2, PART, ROWS)

    def x_part(k, d):
        return parts[k, d]

    zero, one = ring_sum(x_part, x_permute, scales)
    final = [zero[0], zero[1], one[0], one[1]]

    crossed = narrow(jnp.stack(final[1:]), scales).reshape(3, PART, 8, PART)
    crossed = lax.all_to_all(crossed, "pair", split_axis=2, concat_axis=1, tiled=True)
    crossed = crossed.reshape(3, ROWS, PART)

    swapped = aux_permute(after(narrow(one[0], scales), crossed), [(2, 3, 0), (3, 2, 0)])
    lower = [final[0], final[1], jnp.where(x_lo == 1, wide(swapped, scales), final[2]), final[3]]

    back = [
        [(0, 3, -1), (1, 0, 0), (2, 1, 0), (3, 2, 0)],
        [(0, 2, -1), (1, 3, -1), (2, 1, 0), (3, 0, 0)],
        [(0, 1, -1), (1, 2, -1), (2, 3, -1), (3, 0, 0)],
    ]
    upper = [wide(aux_permute(crossed[o], back[o]), scales).T for o in range(3)]
    return jnp.stack(lower[::-1] + upper)


def solution(mesh):
    return jax.shard_map(
        local,
        mesh=mesh,
        in_specs=(P("aux", "pair"), P("pair"), P("pair"), P(), P()),
        out_specs=P(None, ("aux", "pair"), None),
        check_vma=False,
    )
```

```python
import functools

import jax
import jax.numpy as jnp
import numpy as np
from jax import lax
from jax.experimental import pallas as pl
from jax.experimental.pallas import tpu as pltpu
from jax.sharding import PartitionSpec as P

ROWS = 768
HALF = 3072
PART = 96
PLANES = 4
WIDE = 256
freq_point = 0.5

OWN, SIB, FAR_A, FAR_A_SIB, FAR_B, FAR_B_SIB, HALO_A, HALO_B, HALO_A_SIB, HALO_B_SIB, MINOR = range(11)

WHERE = [
    {"A0": OWN, "A1": SIB, "A2": FAR_B, "A3": FAR_A_SIB, "P0": HALO_A, "B3": MINOR},
    {"A1": OWN, "A0": SIB, "A3": FAR_A, "A2": FAR_B_SIB, "P1": HALO_B},
    {"A2": OWN, "A3": SIB, "A0": FAR_A, "A1": FAR_B_SIB, "B2": HALO_B, "B3": HALO_A_SIB, "P0": MINOR},
    {"A3": OWN, "A2": SIB, "A1": FAR_B, "A0": FAR_A_SIB, "B3": HALO_A, "B2": HALO_B_SIB},
]

BATCHES = [
    [["A0A0"],
     ["A1A1"],
     ["A2A2"],
     ["A3A3"]],
    [["P0A1", "P0A3"],
     ["A1A0", "A3A0"],
     ["A0A0", "A0B3"],
     ["A3A2", "A3A0"]],
    [["A3A1"],
     ["A3A3"],
     ["A2B3"],
     ["A2A0"]],
    [["P0A2", "A2A1"],
     ["P1A2", "P1A3"],
     ["P0A1", "A0B2"],
     ["A1A0", "A1A1"]],
    [["A2A2", "A2B3"],
     ["A3A2", "A2A0"],
     ["A2A1", "A3A1"],
     ["A1B3", "A1B2"]],
]
MOVED = [["A0B1", "A0B3", "A0B2", None], [None, None, "A1B2", "A1B3"],
         [None, None, "A0B1", None], [None, None, None, None]]
ENTRIES = [
    [["A0A0", "A0B3", "A0B2", "A0B1"], ["A2A2", "A2A1", "A3A1", "A2B3"]],
    [["A1A1", "A1A0", "A1B3", "A1B2"], ["A3A3", "A3A2", "A2A0", "A3A0"]],
]
def batch_tables(batch, sources):
    held_most = 0
    plans = []
    for role, tiles in enumerate(batch):
        held = []
        first = []
        for step, tile in enumerate(tiles):
            for block in (tile[:2], tile[2:]):
                if block not in held:
                    held.append(block)
                    first.append(step)
        plans.append((held, first))
        held_most = max(held_most, len(held))
    rows = []
    for role, tiles in enumerate(batch):
        held, first = plans[role]
        left = [held.index(tile[:2]) for tile in tiles]
        right = [held.index(tile[2:]) for tile in tiles]
        fresh = [int(i == 0 or left[i] != left[i - 1]) for i in range(len(tiles))]
        pad = held_most - len(held)
        source = [sources.index(WHERE[role][block]) for block in held] + [-1] * pad
        rows.append(left + right + fresh + source + first + [-1] * pad)
    return np.array(rows, np.int32), held_most


def tiles_kernel(count, held_most, sources, table, weight, *refs):
    source_refs = refs[:sources]
    out, held, scaled, sems = refs[sources:]
    step = pl.program_id(0)
    source_at = 3 * count
    first_at = source_at + held_most

    @pl.when(step == 0)
    def _():
        for j in range(held_most):
            for k in range(sources):
                @pl.when(table[source_at + j] == k)
                def _():
                    pltpu.make_async_copy(source_refs[k], held.at[j], sems.at[j]).start()

    def wait(block):
        for j in range(held_most):
            @pl.when((table[first_at + j] == step) & (block == j))
            def _():
                pltpu.make_async_copy(source_refs[0], held.at[j], sems.at[j]).wait()

    left = table[step]
    right = table[count + step]
    wait(left)

    @pl.when(table[2 * count + step] == 1)
    def _():
        @pl.loop(0, ROWS // 32)
        def _(i):
            rows = pl.ds(pl.multiple_of(i * 32, 32), 32)
            scaled[rows, :] = (held[left, rows, :].astype(jnp.float32) * weight[...]).astype(jnp.bfloat16)

    @pl.when(left != right)
    def _():
        wait(right)

    here = table[first_at + held_most]
    for n in range(ROWS // WIDE):
        columns = slice(n * WIDE, (n + 1) * WIDE)
        acc = lax.dot_general(
            scaled[...], held[right, columns, :],
            (((1,), (1,)), ((), ())), preferred_element_type=jnp.float32)
        for y in range(4):
            at = lax.rem(y + 4 - here, 4)
            for h in range(2):
                first = (h * 4 + y) * PART
                out[at, h, 0, :, columns] = acc[first:first + PART]


def tile_batch(batch, table_row, held_most, weight, sources):
    count = len(batch[0])
    return pl.pallas_call(
        functools.partial(tiles_kernel, count, held_most, len(sources)),
        grid_spec=pltpu.PrefetchScalarGridSpec(
            num_scalar_prefetch=1,
            grid=(count,),
            in_specs=[pl.BlockSpec((1, HALF), lambda i, t: (0, 0))]
            + [pl.BlockSpec(memory_space=pl.ANY)] * len(sources),
            out_specs=pl.BlockSpec((4, 2, 1, PART, ROWS), lambda i, t: (0, 0, i, 0, 0)),
            scratch_shapes=[
                pltpu.VMEM((held_most, ROWS, HALF), jnp.bfloat16),
                pltpu.VMEM((ROWS, HALF), jnp.bfloat16),
                pltpu.SemaphoreType.DMA((held_most,)),
            ],
        ),
        out_shape=jax.ShapeDtypeStruct((4, 2, count, PART, ROWS), jnp.float32),
        compiler_params=pltpu.CompilerParams(
            dimension_semantics=("arbitrary",), vmem_limit_bytes=56 * 1024 * 1024),
        cost_estimate=pl.CostEstimate(
            flops=count * ROWS * ROWS,
            bytes_accessed=count * ROWS * ROWS,
            transcendentals=0),
    )(table_row, weight, *sources)


def lookup(table, index):
    blocks = table.shape[0]
    high = lax.shift_right_logical(index, 7)
    low = jnp.bitwise_and(index, 127)
    pairs = index.shape[1]
    hot = jnp.where(lax.broadcasted_iota(jnp.int32, (blocks, pairs), 0) == high, 1.0, 0.0).astype(jnp.bfloat16)
    rest = table
    column = jnp.zeros((128, pairs), jnp.float32)
    for _ in range(3):
        piece = rest.astype(jnp.bfloat16)
        rest = rest - piece.astype(jnp.float32)
        column = column + lax.dot_general(
            piece, hot, (((0,), (0,)), ((), ())), preferred_element_type=jnp.float32)
    mask = lax.broadcasted_iota(jnp.int32, (128, pairs), 0) == low
    return jnp.sum(jnp.where(mask, column, 0.0), axis=0, keepdims=True)


def gap_kernel(occ_index, virt_index, occ_energy, virt_energy, gap):
    gap[...] = lookup(virt_energy[...], virt_index[...]) - lookup(occ_energy[...], occ_index[...])


def pair_gaps(occ_index, virt_index, occ_energy, virt_energy):
    block = 512
    pairs = occ_index.shape[0]
    occ_table = occ_energy.reshape(-1, 128)
    virt_table = virt_energy.reshape(-1, 128)
    line = pl.BlockSpec((1, block), lambda i: (0, i))
    return pl.pallas_call(
        gap_kernel,
        grid=(pairs // block,),
        in_specs=[line, line,
                  pl.BlockSpec(occ_table.shape, lambda i: (0, 0)),
                  pl.BlockSpec(virt_table.shape, lambda i: (0, 0))],
        out_specs=line,
        out_shape=jax.ShapeDtypeStruct((1, pairs), jnp.float32),
        cost_estimate=pl.CostEstimate(flops=6 * 128 * 288 * pairs, bytes_accessed=200000, transcendentals=0),
    )(occ_index[None, :], virt_index[None, :], occ_table, virt_table)


def half_kernel(which, coeffs, half, largest):
    half[...] = coeffs[...]

    @pl.when(pl.program_id(0) == 0)
    def _():
        largest[...] = jnp.zeros_like(largest)

    top = jnp.zeros((coeffs.shape[0], 128), jnp.float32)
    for c in range(HALF // 128):
        top = jnp.maximum(top, jnp.abs(coeffs[:, c * 128:(c + 1) * 128].astype(jnp.float32)))
    largest[...] = jnp.maximum(largest[...], jnp.max(top.reshape(-1, 8, 128), axis=0))


def cut_half(which, coeffs):
    return pl.pallas_call(
        half_kernel,
        grid_spec=pltpu.PrefetchScalarGridSpec(
            num_scalar_prefetch=1,
            grid=(ROWS // PART,),
            in_specs=[pl.BlockSpec((PART, HALF), lambda i, t: (i, t[0]))],
            out_specs=[pl.BlockSpec((PART, HALF), lambda i, t: (i, 0)),
                       pl.BlockSpec((8, 128), lambda i, t: (0, 0))],
        ),
        out_shape=[jax.ShapeDtypeStruct((ROWS, HALF), jnp.bfloat16),
                   jax.ShapeDtypeStruct((8, 128), jnp.float32)],
        compiler_params=pltpu.CompilerParams(vmem_limit_bytes=60 * 1024 * 1024),
        cost_estimate=pl.CostEstimate(flops=0, bytes_accessed=PART * ROWS, transcendentals=0),
    )(which[None], coeffs)


def moves(pairs):
    return [(z * 4 + src, (z + dz) % PLANES * 4 + dst) for z in range(PLANES) for src, dst, dz in pairs]


def aux_permute(value, pairs):
    return lax.ppermute(value, "aux", moves(pairs))


def y_permute(value, by):
    return lax.ppermute(value, "pair", [(h * 4 + y, h * 4 + (y + by) % 4) for h in range(2) for y in range(4)])


def x_permute(value, by, roles=range(4)):
    perm = []
    for z in range(PLANES):
        for x in range(4):
            to = (x + by) % 4
            for core in range(2):
                if x % 2 * 2 + core not in roles:
                    continue
                for y in range(4):
                    source = (z * 4 + x % 2 * 2 + core) * 8 + x // 2 * 4 + y
                    perm.append((source, (z * 4 + to % 2 * 2 + core) * 8 + to // 2 * 4 + y))
    return lax.ppermute(value, ("aux", "pair"), perm)


def both_ways(permute, up, down):
    return lax.optimization_barrier((permute(up, 1), permute(down, -1)))


def ring_sum(part, permute, scales):
    count = part(0, 0).shape[0]
    up, down = both_ways(permute, narrow(jnp.concatenate([part(2, 0), part(1, 1)]), scales),
                         narrow(jnp.concatenate([part(2, 1), part(3, 0)]), scales))
    up_more, down_more = both_ways(permute, narrow(part(1, 0) + wide(up[:count], scales), scales),
                                   narrow(part(3, 1) + wide(down[:count], scales), scales))
    zero = part(0, 0) + wide(down[count:], scales) + wide(up_more, scales)
    one = part(0, 1) + wide(up[count:], scales) + wide(down_more, scales)
    return zero, one


def slot_names(role):
    names = []
    first, second, *rest = [batch[role] for batch in BATCHES]
    for tiles in [first + second] + rest:
        names += [(tile, h) for h in range(2) for tile in tiles]
    early, late = MOVED[role][:2], MOVED[role][2:]
    names += [(tile, h) for h in range(2) for tile in early]
    names += [(tile, h) for h in range(2) for tile in late]
    return names


def entry_table():
    rows = []
    for role in range(4):
        names = slot_names(role)
        for x_hi in range(2):
            row = []
            for k in range(4):
                to = (x_hi * 2 + role // 2 + k) % 4
                row += [names.index((tile, to // 2)) for tile in ENTRIES[role % 2][to % 2]]
            rows.append(row)
    return np.array(rows, np.int32)


def pick_kernel(table, slots, parts):
    for i in range(16):
        parts[i] = slots[table[i]]


def pick_parts(table, slots):
    return pl.pallas_call(
        pick_kernel,
        in_specs=[pl.BlockSpec(memory_space=pltpu.SMEM), pl.BlockSpec(memory_space=pltpu.VMEM)],
        out_specs=pl.BlockSpec(memory_space=pltpu.VMEM),
        out_shape=jax.ShapeDtypeStruct((16, PART, ROWS), jnp.float32),
        compiler_params=pltpu.CompilerParams(vmem_limit_bytes=20 * 1024 * 1024),
        cost_estimate=pl.CostEstimate(flops=0, bytes_accessed=PART * ROWS, transcendentals=0),
    )(table, slots)


def largest_round(value, permute):
    got = [permute(value, by) for by in (1, 2, 3)]
    return jnp.maximum(jnp.maximum(value, got[0]), jnp.maximum(got[1], got[2]))


def scales_of(largest):
    bound = 8.0 * HALF * 4 * largest * largest * 4.0
    scale = 32768.0 / jnp.maximum(bound, 1e-30)
    return scale, 1.0 / scale


def narrow(value, scales):
    return (value * scales[0]).astype(jnp.float16)


def wide(value, scales):
    return value.astype(jnp.float32) * scales[1]


def after(value, other):
    return lax.optimization_barrier((value, other))[0]


def local(coeffs, occ_index, virt_index, occ_energy, virt_energy):
    role = lax.rem(lax.axis_index("aux"), 4)
    x_lo = role // 2
    x_hi = lax.axis_index("pair") // 4
    y = lax.rem(lax.axis_index("pair"), 4)

    which = x_lo.astype(jnp.int32)
    mine, largest = cut_half(which, coeffs)
    which, mine, largest = lax.optimization_barrier((which, mine, largest))
    other, larger = cut_half(1 - which, coeffs)
    largest = jnp.maximum(largest, larger)
    halo_a = aux_permute(mine, [(0, 0, -1), (3, 3, 1)])
    far_a = aux_permute(other, [(0, 2, 0), (3, 1, 0)])
    sib = aux_permute(mine, [(0, 1, 0), (1, 0, 0), (2, 3, 0), (3, 2, 0)])

    largest = jnp.maximum(largest, aux_permute(largest, [(0, 1, 0), (1, 0, 0), (2, 3, 0), (3, 2, 0)]))
    largest = largest_round(largest, y_permute)
    largest = jnp.maximum(largest, x_permute(largest, 2, (1, 2)))
    largest = jnp.maximum(largest, aux_permute(largest, [(1, 2, 0), (2, 1, 0)]))
    largest = jnp.maximum(largest, aux_permute(largest, [(1, 1, 2), (2, 2, 2)]))
    largest = jnp.maximum(largest, aux_permute(largest, [(1, 1, 1), (2, 2, 1)]))
    largest = jnp.maximum(largest, aux_permute(largest, [(1, 0, 0), (2, 3, 0)]))
    scales = scales_of(jnp.max(largest))

    occ_index, virt_index = after([occ_index, virt_index], largest)
    begin = x_lo * HALF
    gap = pair_gaps(
        lax.dynamic_slice_in_dim(occ_index, begin, HALF),
        lax.dynamic_slice_in_dim(virt_index, begin, HALF),
        occ_energy, virt_energy)
    weight = -4.0 * gap / (gap * gap + freq_point * freq_point)

    plans = []
    for batch in BATCHES:
        used = sorted({WHERE[r][t[i:i + 2]] for r in range(4) for t in batch[r] for i in (0, 2)})
        table, held_most = batch_tables(batch, used)
        row = lax.dynamic_index_in_dim(jnp.asarray(table), role, axis=0, keepdims=False)
        row = jnp.concatenate([row, y[None].astype(jnp.int32)])
        plans.append([used, row, held_most])
    entries = lax.dynamic_index_in_dim(jnp.asarray(entry_table()), role * 2 + x_hi, axis=0, keepdims=False)
    rows = [plan[1] for plan in plans]
    held = {OWN: mine}

    def tiles(number):
        used, _, held_most = plans[number]
        return tile_batch(BATCHES[number], rows[number], held_most, weight, [held[s] for s in used])

    def part(partials, k, d):
        return jnp.concatenate([partial[k, d] for partial in partials])

    def first_sends(partials):
        return [narrow(jnp.concatenate([part(partials, 2, 0), part(partials, 1, 1)]), scales),
                narrow(jnp.concatenate([part(partials, 2, 1), part(partials, 3, 0)]), scales)]

    def first_round(sends):
        return [y_permute(sends[0], 1), y_permute(sends[1], -1)]

    def second_sends(partials, got):
        count = got[0].shape[0] // 2
        return [narrow(part(partials, 1, 0) + wide(got[0][:count], scales), scales),
                narrow(part(partials, 3, 1) + wide(got[1][:count], scales), scales)]

    def finish(partials, got, more):
        count = more[0].shape[0]
        zero = part(partials, 0, 0) + wide(got[1][count:], scales) + wide(more[0], scales)
        one = part(partials, 0, 1) + wide(got[0][count:], scales) + wide(more[1], scales)
        return [zero, one]

    alone = tiles(0)
    far_a, sib, scales, weight, entries, rows, alone = lax.optimization_barrier(
        (far_a, sib, scales, weight, entries, rows, alone))

    far_b = aux_permute(after(other, far_a), [(1, 3, 0), (2, 0, 0)])
    minor = aux_permute(far_a, [(1, 0, 1), (2, 2, -1)])
    far_a_sib = aux_permute(far_a, [(1, 0, 0), (2, 3, 0)])
    halo_b = aux_permute(after(mine, halo_a), [(1, 1, -1), (2, 2, 1)])
    halo_a_sib = aux_permute(halo_a, [(3, 2, 0)])
    held.update({SIB: sib, FAR_A: far_a, FAR_A_SIB: far_a_sib, HALO_A: halo_a, HALO_A_SIB: halo_a_sib})

    partial0 = [alone, tiles(1)]
    sends0 = first_sends(partial0)
    got0 = first_round(sends0)
    far_b, minor, rows = lax.optimization_barrier((far_b, minor, rows, got0))[:3]
    held[FAR_B], held[HALO_B], held[MINOR] = far_b, halo_b, minor
    held[FAR_B_SIB] = aux_permute(far_b, [(0, 1, 0), (3, 2, 0)])
    held[HALO_B_SIB] = aux_permute(halo_b, [(2, 3, 0)])
    partial1 = [tiles(2)]
    sends1 = first_sends(partial1)
    got0, sends1 = lax.optimization_barrier((got0, sends1))
    got1 = first_round(sends1)
    more0 = first_round(second_sends(partial0, got0))
    more1 = first_round(second_sends(partial1, got1))
    partial2 = [tiles(3)]
    sends2 = first_sends(partial2)
    got2 = first_round(sends2)
    rows[4], more0 = lax.optimization_barrier((rows[4], more0, sends2))[:2]
    partial3 = [tiles(4)]
    sends3 = first_sends(partial3)
    got2 = after(got2, partial3)
    sends2 = second_sends(partial2, got2)
    more2 = first_round(sends2)
    sends3 = after(sends3, sends2)
    got3 = first_round(sends3)
    more0, more1 = after([more0, more1], sends3)
    total0 = finish(partial0, got0, more0)
    total1 = finish(partial1, got1, more1)
    moved0 = narrow(jnp.concatenate([total0[0][1:], total0[1][1:]]), scales)
    moved0 = aux_permute(moved0, [(0, 0, 1)])
    more2 = after(more2, sends3)
    total2 = finish(partial2, got2, more2)
    moved2 = narrow(jnp.concatenate(total2), scales)
    moved2 = aux_permute(moved2, [(0, 0, 1), (1, 1, 1), (2, 2, 1)])
    got3, moved2, moved0 = lax.optimization_barrier((got3, moved2, moved0))
    more3 = both_ways(y_permute, *second_sends(partial3, got3))
    moved0, moved2 = wide(moved0, scales), wide(moved2, scales)
    total3 = finish(partial3, got3, more3)
    slots = jnp.concatenate(total0 + total1 + total2 + total3 + [moved0, moved2])
    parts = pick_parts(entries, slots).reshape(4, 2, 2, PART, ROWS)

    def x_part(k, d):
        return parts[k, d]

    zero, one = ring_sum(x_part, x_permute, scales)
    final = [zero[0], zero[1], one[0], one[1]]

    crossed = narrow(jnp.stack(final[1:]), scales).reshape(3, PART, 8, PART)
    crossed = lax.all_to_all(crossed, "pair", split_axis=2, concat_axis=1, tiled=True)
    crossed = crossed.reshape(3, ROWS, PART)

    swapped = aux_permute(after(narrow(one[0], scales), crossed), [(2, 3, 0), (3, 2, 0)])
    lower = [final[0], final[1], jnp.where(x_lo == 1, wide(swapped, scales), final[2]), final[3]]

    back = [
        [(0, 3, -1), (1, 0, 0), (2, 1, 0), (3, 2, 0)],
        [(0, 2, -1), (1, 3, -1), (2, 1, 0), (3, 0, 0)],
        [(0, 1, -1), (1, 2, -1), (2, 3, -1), (3, 0, 0)],
    ]
    upper = [wide(aux_permute(crossed[o], back[o]), scales).T for o in range(3)]
    return jnp.stack(lower[::-1] + upper)


def solution(mesh):
    return jax.shard_map(
        local,
        mesh=mesh,
        in_specs=(P("aux", "pair"), P("pair"), P("pair"), P(), P()),
        out_specs=P(None, ("aux", "pair"), None),
        check_vma=False,
    )
```

```python
import functools

import jax
import jax.numpy as jnp
import numpy as np
from jax import lax
from jax.experimental import pallas as pl
from jax.experimental.pallas import tpu as pltpu
from jax.sharding import PartitionSpec as P

ROWS = 768
HALF = 3072
PART = 96
PLANES = 4
WIDE = 256
freq_point = 0.5

OWN, SIB, FAR_A, FAR_A_SIB, FAR_B, FAR_B_SIB, HALO_A, HALO_B, HALO_A_SIB, HALO_B_SIB, MINOR = range(11)

WHERE = [
    {"A0": OWN, "A1": SIB, "A2": FAR_B, "A3": FAR_A_SIB, "P0": HALO_A, "B3": MINOR},
    {"A1": OWN, "A0": SIB, "A3": FAR_A, "A2": FAR_B_SIB, "P1": HALO_B},
    {"A2": OWN, "A3": SIB, "A0": FAR_A, "A1": FAR_B_SIB, "B2": HALO_B, "B3": HALO_A_SIB, "P0": MINOR},
    {"A3": OWN, "A2": SIB, "A1": FAR_B, "A0": FAR_A_SIB, "B3": HALO_A, "B2": HALO_B_SIB},
]

BATCHES = [
    [["A0A0", "P0A1"],
     ["A1A0", "A1A1"],
     ["A2A2", "A0A0"],
     ["A3A2", "A3A3"]],
    [["A3A1", "P0A3"],
     ["A3A0", "A3A3"],
     ["A0B3", "A2B3"],
     ["A3A0", "A2A0"]],
    [["P0A2", "A2A1"],
     ["P1A2", "P1A3"],
     ["P0A1", "A0B2"],
     ["A1A0", "A1A1"]],
    [["A2A2", "A2B3"],
     ["A3A2", "A2A0"],
     ["A2A1", "A3A1"],
     ["A1B3", "A1B2"]],
]
MOVED = [["A0B1", "A0B3", "A0B2", None], [None, None, "A1B2", "A1B3"],
         [None, None, "A0B1", None], [None, None, None, None]]
ENTRIES = [
    [["A0A0", "A0B3", "A0B2", "A0B1"], ["A2A2", "A2A1", "A3A1", "A2B3"]],
    [["A1A1", "A1A0", "A1B3", "A1B2"], ["A3A3", "A3A2", "A2A0", "A3A0"]],
]
ORDER = [(2, 0), (1, 1), (2, 1), (3, 0), (0, 0), (0, 1), (1, 0), (3, 1)]
ROW_ORDER = np.array([[ORDER.index(((rows % 4 - y) % 4, rows // 4)) for rows in range(8)] for y in range(4)], np.int32)


def batch_tables(batch, sources):
    held_most = 0
    plans = []
    for role, tiles in enumerate(batch):
        held = []
        first = []
        for step, tile in enumerate(tiles):
            for block in (tile[:2], tile[2:]):
                if block not in held:
                    held.append(block)
                    first.append(step)
        plans.append((held, first))
        held_most = max(held_most, len(held))
    rows = []
    for role, tiles in enumerate(batch):
        held, first = plans[role]
        left = [held.index(tile[:2]) for tile in tiles]
        right = [held.index(tile[2:]) for tile in tiles]
        fresh = [int(i == 0 or left[i] != left[i - 1]) for i in range(len(tiles))]
        pad = held_most - len(held)
        source = [sources.index(WHERE[role][block]) for block in held] + [-1] * pad
        rows.append(left + right + fresh + source + first + [-1] * pad)
    return np.array(rows, np.int32), held_most


def tiles_kernel(count, held_most, sources, table, weight, *refs):
    source_refs = refs[:sources]
    out, held, scaled, sems = refs[sources:]
    step = pl.program_id(0)
    source_at = 3 * count
    first_at = source_at + held_most

    def fetch(of_first):
        for j in range(held_most):
            for k in range(sources):
                @pl.when((table[source_at + j] == k) & ((table[first_at + j] == 0) == of_first))
                def _():
                    pltpu.make_async_copy(source_refs[k], held.at[j], sems.at[j]).start()

    @pl.when(step == 0)
    def _():
        fetch(True)

    def wait(block):
        for j in range(held_most):
            @pl.when((table[first_at + j] == step) & (block == j))
            def _():
                pltpu.make_async_copy(source_refs[0], held.at[j], sems.at[j]).wait()

    left = table[step]
    right = table[count + step]
    wait(left)

    @pl.when(table[2 * count + step] == 1)
    def _():
        @pl.loop(0, ROWS // 32)
        def _(i):
            rows = pl.ds(pl.multiple_of(i * 32, 32), 32)
            scaled[rows, :] = (held[left, rows, :].astype(jnp.float32) * weight[...]).astype(jnp.bfloat16)

    @pl.when(left != right)
    def _():
        wait(right)

    @pl.when(step == 0)
    def _():
        fetch(False)

    order_at = first_at + held_most
    for n in range(ROWS // WIDE):
        columns = slice(n * WIDE, (n + 1) * WIDE)
        acc = lax.dot_general(
            scaled[...], held[right, columns, :],
            (((1,), (1,)), ((), ())), preferred_element_type=jnp.float32)
        for rows in range(8):
            out[table[order_at + rows], 0, :, columns] = acc[rows * PART:(rows + 1) * PART]


def tile_batch(batch, table_row, held_most, weight, sources):
    count = len(batch[0])
    return pl.pallas_call(
        functools.partial(tiles_kernel, count, held_most, len(sources)),
        grid_spec=pltpu.PrefetchScalarGridSpec(
            num_scalar_prefetch=1,
            grid=(count,),
            in_specs=[pl.BlockSpec((1, HALF), lambda i, t: (0, 0))]
            + [pl.BlockSpec(memory_space=pl.ANY)] * len(sources),
            out_specs=pl.BlockSpec((8, 1, PART, ROWS), lambda i, t: (0, i, 0, 0)),
            scratch_shapes=[
                pltpu.VMEM((held_most, ROWS, HALF), jnp.bfloat16),
                pltpu.VMEM((ROWS, HALF), jnp.bfloat16),
                pltpu.SemaphoreType.DMA((held_most,)),
            ],
        ),
        out_shape=jax.ShapeDtypeStruct((8, count, PART, ROWS), jnp.float32),
        compiler_params=pltpu.CompilerParams(
            dimension_semantics=("arbitrary",), vmem_limit_bytes=56 * 1024 * 1024),
        cost_estimate=pl.CostEstimate(
            flops=count * ROWS * ROWS,
            bytes_accessed=count * ROWS * ROWS,
            transcendentals=0),
    )(table_row, weight, *sources)


def lookup(table, index):
    blocks = table.shape[0]
    high = lax.shift_right_logical(index, 7)
    low = jnp.bitwise_and(index, 127)
    pairs = index.shape[1]
    hot = jnp.where(lax.broadcasted_iota(jnp.int32, (blocks, pairs), 0) == high, 1.0, 0.0).astype(jnp.bfloat16)
    rest = table
    column = jnp.zeros((128, pairs), jnp.float32)
    for _ in range(3):
        piece = rest.astype(jnp.bfloat16)
        rest = rest - piece.astype(jnp.float32)
        column = column + lax.dot_general(
            piece, hot, (((0,), (0,)), ((), ())), preferred_element_type=jnp.float32)
    mask = lax.broadcasted_iota(jnp.int32, (128, pairs), 0) == low
    return jnp.sum(jnp.where(mask, column, 0.0), axis=0, keepdims=True)


def gap_kernel(occ_index, virt_index, occ_energy, virt_energy, gap):
    gap[...] = lookup(virt_energy[...], virt_index[...]) - lookup(occ_energy[...], occ_index[...])


def pair_gaps(occ_index, virt_index, occ_energy, virt_energy):
    block = 512
    pairs = occ_index.shape[0]
    occ_table = occ_energy.reshape(-1, 128)
    virt_table = virt_energy.reshape(-1, 128)
    line = pl.BlockSpec((1, block), lambda i: (0, i))
    return pl.pallas_call(
        gap_kernel,
        grid=(pairs // block,),
        in_specs=[line, line,
                  pl.BlockSpec(occ_table.shape, lambda i: (0, 0)),
                  pl.BlockSpec(virt_table.shape, lambda i: (0, 0))],
        out_specs=line,
        out_shape=jax.ShapeDtypeStruct((1, pairs), jnp.float32),
        cost_estimate=pl.CostEstimate(flops=6 * 128 * 288 * pairs, bytes_accessed=200000, transcendentals=0),
    )(occ_index[None, :], virt_index[None, :], occ_table, virt_table)


def halves_kernel(x_lo, coeffs, mine, other, largest):
    for low in range(2):
        @pl.when(x_lo[0] == low)
        def _():
            mine[...] = coeffs[:, low * HALF:(low + 1) * HALF]
            other[...] = coeffs[:, (1 - low) * HALF:(2 - low) * HALF]

    @pl.when(pl.program_id(0) == 0)
    def _():
        largest[...] = jnp.zeros_like(largest)

    top = jnp.zeros((coeffs.shape[0], 128), jnp.float32)
    for c in range(coeffs.shape[1] // 128):
        top = jnp.maximum(top, jnp.abs(coeffs[:, c * 128:(c + 1) * 128].astype(jnp.float32)))
    largest[...] = jnp.maximum(largest[...], jnp.max(top.reshape(-1, 8, 128), axis=0))


def cut_in_halves(x_lo, coeffs):
    half = jax.ShapeDtypeStruct((ROWS, HALF), jnp.bfloat16)
    block = pl.BlockSpec((PART, HALF), lambda i, t: (i, 0))
    return pl.pallas_call(
        halves_kernel,
        grid_spec=pltpu.PrefetchScalarGridSpec(
            num_scalar_prefetch=1,
            grid=(ROWS // PART,),
            in_specs=[pl.BlockSpec((PART, 2 * HALF), lambda i, t: (i, 0))],
            out_specs=[block, block, pl.BlockSpec((8, 128), lambda i, t: (0, 0))],
        ),
        out_shape=[half, half, jax.ShapeDtypeStruct((8, 128), jnp.float32)],
        compiler_params=pltpu.CompilerParams(vmem_limit_bytes=24 * 1024 * 1024),
        cost_estimate=pl.CostEstimate(flops=0, bytes_accessed=PART * ROWS, transcendentals=0),
    )(x_lo[None], coeffs)


def moves(pairs):
    return [(z * 4 + src, (z + dz) % PLANES * 4 + dst) for z in range(PLANES) for src, dst, dz in pairs]


def aux_permute(value, pairs):
    return lax.ppermute(value, "aux", moves(pairs))


def y_permute(value, by):
    return lax.ppermute(value, "pair", [(h * 4 + y, h * 4 + (y + by) % 4) for h in range(2) for y in range(4)])


def x_permute(value, by, roles=range(4)):
    perm = []
    for z in range(PLANES):
        for x in range(4):
            to = (x + by) % 4
            for core in range(2):
                if x % 2 * 2 + core not in roles:
                    continue
                for y in range(4):
                    source = (z * 4 + x % 2 * 2 + core) * 8 + x // 2 * 4 + y
                    perm.append((source, (z * 4 + to % 2 * 2 + core) * 8 + to // 2 * 4 + y))
    return lax.ppermute(value, ("aux", "pair"), perm)


def both_ways(permute, up, down):
    return lax.optimization_barrier((permute(up, 1), permute(down, -1)))


def first_sends(terms, scales):
    return [narrow(terms[0:2], scales), narrow(terms[2:4], scales)]


def second_sends(terms, got, scales):
    return [narrow(terms[6] + wide(got[0][0], scales), scales),
            narrow(terms[7] + wide(got[1][0], scales), scales)]


def finish(terms, got, more, scales, slots=slice(None)):
    zero = terms[4][slots] + wide(got[1][1][slots], scales) + wide(more[0][slots], scales)
    one = terms[5][slots] + wide(got[0][1][slots], scales) + wide(more[1][slots], scales)
    return [zero, one]


def slot_names(role):
    names = []
    for batch in BATCHES:
        names += [(tile, h) for h in range(2) for tile in batch[role]]
    early, late = MOVED[role][:2], MOVED[role][2:]
    names += [(tile, h) for h in range(2) for tile in early]
    names += [(tile, h) for h in range(2) for tile in late]
    return names


def entry_table():
    rows = []
    for role in range(4):
        names = slot_names(role)
        for x_hi in range(2):
            row = []
            for k, d in ORDER:
                to = (x_hi * 2 + role // 2 + k) % 4
                row += [names.index((tile, to // 2)) for tile in ENTRIES[role % 2][to % 2][2 * d:2 * d + 2]]
            rows.append(row)
    return np.array(rows, np.int32)


def pick_kernel(table, slots, parts):
    for i in range(16):
        parts[i] = slots[table[i]]


def pick_parts(table, slots):
    return pl.pallas_call(
        pick_kernel,
        in_specs=[pl.BlockSpec(memory_space=pltpu.SMEM), pl.BlockSpec(memory_space=pltpu.VMEM)],
        out_specs=pl.BlockSpec(memory_space=pltpu.VMEM),
        out_shape=jax.ShapeDtypeStruct((16, PART, ROWS), jnp.float32),
        compiler_params=pltpu.CompilerParams(vmem_limit_bytes=20 * 1024 * 1024),
        cost_estimate=pl.CostEstimate(flops=0, bytes_accessed=PART * ROWS, transcendentals=0),
    )(table, slots)


def largest_round(value, permute):
    got = [permute(value, by) for by in (1, 2, 3)]
    return jnp.maximum(jnp.maximum(value, got[0]), jnp.maximum(got[1], got[2]))


def scales_of(largest):
    bound = 8.0 * HALF * 4 * largest * largest * 4.0
    scale = 32768.0 / jnp.maximum(bound, 1e-30)
    return scale, 1.0 / scale


def narrow(value, scales):
    return (value * scales[0]).astype(jnp.float16)


def wide(value, scales):
    return value.astype(jnp.float32) * scales[1]


def after(value, other):
    return lax.optimization_barrier((value, other))[0]


def local(coeffs, occ_index, virt_index, occ_energy, virt_energy):
    role = lax.rem(lax.axis_index("aux"), 4)
    x_lo = role // 2
    x_hi = lax.axis_index("pair") // 4
    y = lax.rem(lax.axis_index("pair"), 4)

    mine, other, largest = cut_in_halves(x_lo.astype(jnp.int32), coeffs)
    halo_a = aux_permute(mine, [(0, 0, -1), (3, 3, 1)])
    far_a = aux_permute(other, [(0, 2, 0), (3, 1, 0)])
    sib = aux_permute(mine, [(0, 1, 0), (1, 0, 0), (2, 3, 0), (3, 2, 0)])

    largest = jnp.maximum(largest, aux_permute(largest, [(0, 1, 0), (1, 0, 0), (2, 3, 0), (3, 2, 0)]))
    largest = largest_round(largest, y_permute)
    largest = jnp.maximum(largest, x_permute(largest, 2, (1, 2)))
    largest = jnp.maximum(largest, aux_permute(largest, [(1, 2, 0), (2, 1, 0)]))
    largest = jnp.maximum(largest, aux_permute(largest, [(1, 1, 2), (2, 2, 2)]))
    largest = jnp.maximum(largest, aux_permute(largest, [(1, 1, 1), (2, 2, 1)]))
    largest = jnp.maximum(largest, aux_permute(largest, [(1, 0, 0), (2, 3, 0)]))
    scales = scales_of(jnp.max(largest))

    occ_index, virt_index = after([occ_index, virt_index], mine)
    begin = x_lo * HALF
    gap = pair_gaps(
        lax.dynamic_slice_in_dim(occ_index, begin, HALF),
        lax.dynamic_slice_in_dim(virt_index, begin, HALF),
        occ_energy, virt_energy)
    weight = -4.0 * gap / (gap * gap + freq_point * freq_point)

    plans = []
    for batch in BATCHES:
        used = sorted({WHERE[r][t[i:i + 2]] for r in range(4) for t in batch[r] for i in (0, 2)})
        table, held_most = batch_tables(batch, used)
        row = lax.dynamic_index_in_dim(jnp.asarray(table), role, axis=0, keepdims=False)
        row = jnp.concatenate([row, lax.dynamic_index_in_dim(jnp.asarray(ROW_ORDER), y, axis=0, keepdims=False)])
        plans.append([used, row, held_most])
    entries = lax.dynamic_index_in_dim(jnp.asarray(entry_table()), role * 2 + x_hi, axis=0, keepdims=False)
    rows = [plan[1] for plan in plans]
    halo_a, far_a, sib, scales, weight, entries, rows = lax.optimization_barrier(
        (halo_a, far_a, sib, scales, weight, entries, rows))

    far_b = aux_permute(after(other, far_a), [(1, 3, 0), (2, 0, 0)])
    halo_b = aux_permute(after(mine, halo_a), [(1, 1, -1), (2, 2, 1)])
    far_a_sib = aux_permute(far_a, [(1, 0, 0), (2, 3, 0)])
    halo_a_sib = aux_permute(halo_a, [(3, 2, 0)])
    minor = aux_permute(far_a, [(1, 0, 1), (2, 2, -1)])

    held = {OWN: mine, SIB: sib, FAR_A: far_a, HALO_A: halo_a}

    def tiles(number):
        used, _, held_most = plans[number]
        return tile_batch(BATCHES[number], rows[number], held_most, weight, [held[s] for s in used])

    def first_round(sends):
        return [y_permute(sends[0], 1), y_permute(sends[1], -1)]

    partial0 = tiles(0)
    sends0 = first_sends(partial0, scales)
    held[FAR_A_SIB], held[HALO_A_SIB] = after([far_a_sib, halo_a_sib], sends0)
    got0 = first_round(sends0)
    partial1 = tiles(1)
    sends1 = first_sends(partial1, scales)
    got0, sends1 = lax.optimization_barrier((got0, sends1))
    got1 = first_round(sends1)
    more = second_sends(partial0, got0, scales)
    minor, far_b, halo_b, got1, more = lax.optimization_barrier((minor, far_b, halo_b, got1, more))
    held[FAR_B], held[HALO_B], held[MINOR] = far_b, halo_b, minor
    held[FAR_B_SIB] = aux_permute(far_b, [(0, 1, 0), (3, 2, 0)])
    held[HALO_B_SIB] = aux_permute(halo_b, [(2, 3, 0)])
    more = [jnp.concatenate(pair) for pair in zip(more, second_sends(partial1, got1, scales))]
    more = first_round(more)
    partial2 = tiles(2)
    sends2 = first_sends(partial2, scales)
    got2 = first_round(sends2)
    more = after(more, sends2)
    more0, more1 = [m[:2] for m in more], [m[2:] for m in more]
    moved0 = [finish(partial0, got0, more0, scales, slice(1, 2)), finish(partial1, got1, more1, scales, slice(1, 2))]
    moved0 = narrow(jnp.concatenate([tile[h] for h in range(2) for tile in moved0]), scales)
    rows[3], moved0 = lax.optimization_barrier((rows[3], moved0, sends2))[:2]
    moved0 = aux_permute(moved0, [(0, 0, 1)])
    partial3 = tiles(3)
    sends3 = first_sends(partial3, scales)
    got2 = after(got2, partial3)
    sends2 = second_sends(partial2, got2, scales)
    more2 = first_round(sends2)
    sends3 = after(sends3, sends2)
    got3 = first_round(sends3)
    more2 = after(more2, sends3)
    total2 = finish(partial2, got2, more2, scales)
    moved2 = narrow(jnp.concatenate(total2), scales)
    more0, more1 = after([more0, more1], moved2)
    total0 = finish(partial0, got0, more0, scales)
    total1 = finish(partial1, got1, more1, scales)
    moved2 = aux_permute(moved2, [(0, 0, 1), (1, 1, 1), (2, 2, 1)])
    got3, moved2, moved0 = lax.optimization_barrier((got3, moved2, moved0))
    more3 = both_ways(y_permute, *second_sends(partial3, got3, scales))
    moved0, moved2 = wide(moved0, scales), wide(moved2, scales)
    total3 = finish(partial3, got3, more3, scales)
    slots = jnp.concatenate(total0 + total1 + total2 + total3 + [moved0, moved2])
    terms = pick_parts(entries, slots).reshape(8, 2, PART, ROWS)
    got = both_ways(x_permute, *first_sends(terms, scales))
    zero, one = finish(terms, got, both_ways(x_permute, *second_sends(terms, got, scales)), scales)
    final = [zero[0], zero[1], one[0], one[1]]

    crossed = narrow(jnp.stack(final[1:]), scales).reshape(3, PART, 8, PART)
    crossed = lax.all_to_all(crossed, "pair", split_axis=2, concat_axis=1, tiled=True)
    crossed = crossed.reshape(3, ROWS, PART)

    swapped = aux_permute(after(narrow(one[0], scales), crossed), [(2, 3, 0), (3, 2, 0)])
    lower = [final[0], final[1], jnp.where(x_lo == 1, wide(swapped, scales), final[2]), final[3]]

    back = [
        [(0, 3, -1), (1, 0, 0), (2, 1, 0), (3, 2, 0)],
        [(0, 2, -1), (1, 3, -1), (2, 1, 0), (3, 0, 0)],
        [(0, 1, -1), (1, 2, -1), (2, 3, -1), (3, 0, 0)],
    ]
    upper = [wide(aux_permute(crossed[o], back[o]), scales).T for o in range(3)]
    return jnp.stack(lower[::-1] + upper)


def solution(mesh):
    return jax.shard_map(
        local,
        mesh=mesh,
        in_specs=(P("aux", "pair"), P("pair"), P("pair"), P(), P()),
        out_specs=P(None, ("aux", "pair"), None),
        check_vma=False,
    )
```

```python
import functools

import jax
import jax.numpy as jnp
import numpy as np
from jax import lax
from jax.experimental import pallas as pl
from jax.experimental.pallas import tpu as pltpu
from jax.sharding import PartitionSpec as P

ROWS = 768
HALF = 3072
PART = 96
PLANES = 4
WIDE = 256
freq_point = 0.5

OWN, SIB, FAR_A, FAR_A_SIB, FAR_B, FAR_B_SIB, HALO_A, HALO_B, HALO_A_SIB, HALO_B_SIB, MINOR = range(11)

WHERE = [
    {"A0": OWN, "A1": SIB, "A2": FAR_B, "A3": FAR_A_SIB, "P0": HALO_A, "B3": MINOR},
    {"A1": OWN, "A0": SIB, "A3": FAR_A, "A2": FAR_B_SIB, "P1": HALO_B},
    {"A2": OWN, "A3": SIB, "A0": FAR_A, "A1": FAR_B_SIB, "B2": HALO_B, "B3": HALO_A_SIB, "P0": MINOR},
    {"A3": OWN, "A2": SIB, "A1": FAR_B, "A0": FAR_A_SIB, "B3": HALO_A, "B2": HALO_B_SIB},
]

BATCHES = [
    [["A0A0", "P0A1"],
     ["A1A0", "A1A1"],
     ["A2A2", "A0A0"],
     ["A3A2", "A3A3"]],
    [["A3A1", "P0A3"],
     ["A3A0", "A3A3"],
     ["A0B3", "A2B3"],
     ["A3A0", "A2A0"]],
    [["P0A2", "A2A1"],
     ["P1A2", "P1A3"],
     ["P0A1", "A0B2"],
     ["A1A0", "A1A1"]],
    [["A2A2", "A2B3"],
     ["A3A2", "A2A0"],
     ["A2A1", "A3A1"],
     ["A1B3", "A1B2"]],
]
MOVED = [["A0B1", "A0B3", "A0B2", None], [None, None, "A1B2", "A1B3"],
         [None, None, "A0B1", None], [None, None, None, None]]
ENTRIES = [
    [["A0A0", "A0B3", "A0B2", "A0B1"], ["A2A2", "A2A1", "A3A1", "A2B3"]],
    [["A1A1", "A1A0", "A1B3", "A1B2"], ["A3A3", "A3A2", "A2A0", "A3A0"]],
]
ORDER = [(2, 0), (1, 1), (2, 1), (3, 0), (0, 0), (0, 1), (1, 0), (3, 1)]
ROW_ORDER = np.array([[ORDER.index(((rows % 4 - y) % 4, rows // 4)) for rows in range(8)] for y in range(4)], np.int32)


def batch_tables(batch, sources):
    held_most = 0
    plans = []
    for role, tiles in enumerate(batch):
        held = []
        first = []
        for step, tile in enumerate(tiles):
            for block in (tile[:2], tile[2:]):
                if block not in held:
                    held.append(block)
                    first.append(step)
        plans.append((held, first))
        held_most = max(held_most, len(held))
    rows = []
    for role, tiles in enumerate(batch):
        held, first = plans[role]
        left = [held.index(tile[:2]) for tile in tiles]
        right = [held.index(tile[2:]) for tile in tiles]
        fresh = [int(i == 0 or left[i] != left[i - 1]) for i in range(len(tiles))]
        pad = held_most - len(held)
        source = [sources.index(WHERE[role][block]) for block in held] + [-1] * pad
        rows.append(left + right + fresh + source + first + [-1] * pad)
    return np.array(rows, np.int32), held_most


def tiles_kernel(count, held_most, sources, table, weight, *refs):
    source_refs = refs[:sources]
    out, held, scaled, sems = refs[sources:]
    step = pl.program_id(0)
    source_at = 3 * count
    first_at = source_at + held_most

    def fetch(of_first):
        for j in range(held_most):
            for k in range(sources):
                @pl.when((table[source_at + j] == k) & ((table[first_at + j] == 0) == of_first))
                def _():
                    pltpu.make_async_copy(source_refs[k], held.at[j], sems.at[j]).start()

    @pl.when(step == 0)
    def _():
        fetch(True)

    def wait(block):
        for j in range(held_most):
            @pl.when((table[first_at + j] == step) & (block == j))
            def _():
                pltpu.make_async_copy(source_refs[0], held.at[j], sems.at[j]).wait()

    left = table[step]
    right = table[count + step]
    wait(left)

    @pl.when(table[2 * count + step] == 1)
    def _():
        @pl.loop(0, ROWS // 32)
        def _(i):
            rows = pl.ds(pl.multiple_of(i * 32, 32), 32)
            scaled[rows, :] = (held[left, rows, :].astype(jnp.float32) * weight[...]).astype(jnp.bfloat16)

    @pl.when(left != right)
    def _():
        wait(right)

    @pl.when(step == 0)
    def _():
        fetch(False)

    order_at = first_at + held_most
    for n in range(ROWS // WIDE):
        columns = slice(n * WIDE, (n + 1) * WIDE)
        acc = lax.dot_general(
            scaled[...], held[right, columns, :],
            (((1,), (1,)), ((), ())), preferred_element_type=jnp.float32)
        for rows in range(8):
            out[table[order_at + rows], 0, :, columns] = acc[rows * PART:(rows + 1) * PART]


def tile_batch(batch, table_row, held_most, weight, sources):
    count = len(batch[0])
    return pl.pallas_call(
        functools.partial(tiles_kernel, count, held_most, len(sources)),
        grid_spec=pltpu.PrefetchScalarGridSpec(
            num_scalar_prefetch=1,
            grid=(count,),
            in_specs=[pl.BlockSpec((1, HALF), lambda i, t: (0, 0))]
            + [pl.BlockSpec(memory_space=pl.ANY)] * len(sources),
            out_specs=pl.BlockSpec((8, 1, PART, ROWS), lambda i, t: (0, i, 0, 0)),
            scratch_shapes=[
                pltpu.VMEM((held_most, ROWS, HALF), jnp.bfloat16),
                pltpu.VMEM((ROWS, HALF), jnp.bfloat16),
                pltpu.SemaphoreType.DMA((held_most,)),
            ],
        ),
        out_shape=jax.ShapeDtypeStruct((8, count, PART, ROWS), jnp.float32),
        compiler_params=pltpu.CompilerParams(
            dimension_semantics=("arbitrary",), vmem_limit_bytes=36 * 1024 * 1024),
        cost_estimate=pl.CostEstimate(
            flops=count * ROWS * ROWS,
            bytes_accessed=count * ROWS * ROWS,
            transcendentals=0),
    )(table_row, weight, *sources)


def lookup(table, index):
    blocks = table.shape[0]
    high = lax.shift_right_logical(index, 7)
    low = jnp.bitwise_and(index, 127)
    pairs = index.shape[1]
    hot = jnp.where(lax.broadcasted_iota(jnp.int32, (blocks, pairs), 0) == high, 1.0, 0.0).astype(jnp.bfloat16)
    rest = table
    column = jnp.zeros((128, pairs), jnp.float32)
    for _ in range(3):
        piece = rest.astype(jnp.bfloat16)
        rest = rest - piece.astype(jnp.float32)
        column = column + lax.dot_general(
            piece, hot, (((0,), (0,)), ((), ())), preferred_element_type=jnp.float32)
    mask = lax.broadcasted_iota(jnp.int32, (128, pairs), 0) == low
    return jnp.sum(jnp.where(mask, column, 0.0), axis=0, keepdims=True)


def gap_kernel(occ_index, virt_index, occ_energy, virt_energy, gap):
    gap[...] = lookup(virt_energy[...], virt_index[...]) - lookup(occ_energy[...], occ_index[...])


def pair_gaps(occ_index, virt_index, occ_energy, virt_energy):
    block = 512
    pairs = occ_index.shape[0]
    occ_table = occ_energy.reshape(-1, 128)
    virt_table = virt_energy.reshape(-1, 128)
    line = pl.BlockSpec((1, block), lambda i: (0, i))
    return pl.pallas_call(
        gap_kernel,
        grid=(pairs // block,),
        in_specs=[line, line,
                  pl.BlockSpec(occ_table.shape, lambda i: (0, 0)),
                  pl.BlockSpec(virt_table.shape, lambda i: (0, 0))],
        out_specs=line,
        out_shape=jax.ShapeDtypeStruct((1, pairs), jnp.float32),
        cost_estimate=pl.CostEstimate(flops=6 * 128 * 288 * pairs, bytes_accessed=200000, transcendentals=0),
    )(occ_index[None, :], virt_index[None, :], occ_table, virt_table)


def halves_kernel(x_lo, coeffs, mine, other, largest):
    for low in range(2):
        @pl.when(x_lo[0] == low)
        def _():
            mine[...] = coeffs[:, low * HALF:(low + 1) * HALF]
            other[...] = coeffs[:, (1 - low) * HALF:(2 - low) * HALF]

    @pl.when(pl.program_id(0) == 0)
    def _():
        largest[...] = jnp.zeros_like(largest)

    top = jnp.zeros((coeffs.shape[0], 128), jnp.float32)
    for c in range(coeffs.shape[1] // 128):
        top = jnp.maximum(top, jnp.abs(coeffs[:, c * 128:(c + 1) * 128].astype(jnp.float32)))
    largest[...] = jnp.maximum(largest[...], jnp.max(top.reshape(-1, 8, 128), axis=0))


def cut_in_halves(x_lo, coeffs):
    half = jax.ShapeDtypeStruct((ROWS, HALF), jnp.bfloat16)
    block = pl.BlockSpec((PART, HALF), lambda i, t: (i, 0))
    return pl.pallas_call(
        halves_kernel,
        grid_spec=pltpu.PrefetchScalarGridSpec(
            num_scalar_prefetch=1,
            grid=(ROWS // PART,),
            in_specs=[pl.BlockSpec((PART, 2 * HALF), lambda i, t: (i, 0))],
            out_specs=[block, block, pl.BlockSpec((8, 128), lambda i, t: (0, 0))],
        ),
        out_shape=[half, half, jax.ShapeDtypeStruct((8, 128), jnp.float32)],
        compiler_params=pltpu.CompilerParams(vmem_limit_bytes=24 * 1024 * 1024),
        cost_estimate=pl.CostEstimate(flops=0, bytes_accessed=PART * ROWS, transcendentals=0),
    )(x_lo[None], coeffs)


def moves(pairs):
    return [(z * 4 + src, (z + dz) % PLANES * 4 + dst) for z in range(PLANES) for src, dst, dz in pairs]


def aux_permute(value, pairs):
    return lax.ppermute(value, "aux", moves(pairs))


def y_permute(value, by):
    return lax.ppermute(value, "pair", [(h * 4 + y, h * 4 + (y + by) % 4) for h in range(2) for y in range(4)])


def x_permute(value, by, roles=range(4)):
    perm = []
    for z in range(PLANES):
        for x in range(4):
            to = (x + by) % 4
            for core in range(2):
                if x % 2 * 2 + core not in roles:
                    continue
                for y in range(4):
                    source = (z * 4 + x % 2 * 2 + core) * 8 + x // 2 * 4 + y
                    perm.append((source, (z * 4 + to % 2 * 2 + core) * 8 + to // 2 * 4 + y))
    return lax.ppermute(value, ("aux", "pair"), perm)


def both_ways(permute, up, down):
    return lax.optimization_barrier((permute(up, 1), permute(down, -1)))


def first_sends(terms, scales):
    return [narrow(terms[0:2], scales), narrow(terms[2:4], scales)]


def second_sends(terms, got, scales):
    return [narrow(terms[6] + wide(got[0][0], scales), scales),
            narrow(terms[7] + wide(got[1][0], scales), scales)]


def finish(terms, got, more, scales, slots=slice(None)):
    zero = terms[4][slots] + wide(got[1][1][slots], scales) + wide(more[0][slots], scales)
    one = terms[5][slots] + wide(got[0][1][slots], scales) + wide(more[1][slots], scales)
    return [zero, one]


def slot_names(role):
    names = []
    for batch in BATCHES:
        names += [(tile, h) for h in range(2) for tile in batch[role]]
    early, late = MOVED[role][:2], MOVED[role][2:]
    names += [(tile, h) for h in range(2) for tile in early]
    names += [(tile, h) for h in range(2) for tile in late]
    return names


def entry_table():
    rows = []
    for role in range(4):
        names = slot_names(role)
        for x_hi in range(2):
            row = []
            for k, d in ORDER:
                to = (x_hi * 2 + role // 2 + k) % 4
                row += [names.index((tile, to // 2)) for tile in ENTRIES[role % 2][to % 2][2 * d:2 * d + 2]]
            rows.append(row)
    return np.array(rows, np.int32)


def pick_kernel(table, slots, parts):
    for i in range(16):
        parts[i] = slots[table[i]]


def pick_parts(table, slots):
    return pl.pallas_call(
        pick_kernel,
        in_specs=[pl.BlockSpec(memory_space=pltpu.SMEM), pl.BlockSpec(memory_space=pltpu.VMEM)],
        out_specs=pl.BlockSpec(memory_space=pltpu.VMEM),
        out_shape=jax.ShapeDtypeStruct((16, PART, ROWS), jnp.float32),
        compiler_params=pltpu.CompilerParams(vmem_limit_bytes=20 * 1024 * 1024),
        cost_estimate=pl.CostEstimate(flops=0, bytes_accessed=PART * ROWS, transcendentals=0),
    )(table, slots)


def largest_round(value, permute):
    got = [permute(value, by) for by in (1, 2, 3)]
    return jnp.maximum(jnp.maximum(value, got[0]), jnp.maximum(got[1], got[2]))


def scales_of(largest):
    bound = 8.0 * HALF * 4 * largest * largest * 4.0
    scale = 32768.0 / jnp.maximum(bound, 1e-30)
    return scale, 1.0 / scale


def narrow(value, scales):
    return (value * scales[0]).astype(jnp.float16)


def wide(value, scales):
    return value.astype(jnp.float32) * scales[1]


def after(value, other):
    return lax.optimization_barrier((value, other))[0]


def local(coeffs, occ_index, virt_index, occ_energy, virt_energy):
    role = lax.rem(lax.axis_index("aux"), 4)
    x_lo = role // 2
    x_hi = lax.axis_index("pair") // 4
    y = lax.rem(lax.axis_index("pair"), 4)

    mine, other, largest = cut_in_halves(x_lo.astype(jnp.int32), coeffs)
    halo_a = aux_permute(mine, [(0, 0, -1), (3, 3, 1)])
    far_a = aux_permute(other, [(0, 2, 0), (3, 1, 0)])
    sib = aux_permute(mine, [(0, 1, 0), (1, 0, 0), (2, 3, 0), (3, 2, 0)])

    largest = jnp.maximum(largest, aux_permute(largest, [(0, 1, 0), (1, 0, 0), (2, 3, 0), (3, 2, 0)]))
    largest = largest_round(largest, y_permute)
    largest = jnp.maximum(largest, x_permute(largest, 2, (1, 2)))
    largest = jnp.maximum(largest, aux_permute(largest, [(1, 2, 0), (2, 1, 0)]))
    largest = jnp.maximum(largest, aux_permute(largest, [(1, 1, 2), (2, 2, 2)]))
    largest = jnp.maximum(largest, aux_permute(largest, [(1, 1, 1), (2, 2, 1)]))
    largest = jnp.maximum(largest, aux_permute(largest, [(1, 0, 0), (2, 3, 0)]))
    scales = scales_of(jnp.max(largest))

    occ_index, virt_index = after([occ_index, virt_index], mine)
    begin = x_lo * HALF
    gap = pair_gaps(
        lax.dynamic_slice_in_dim(occ_index, begin, HALF),
        lax.dynamic_slice_in_dim(virt_index, begin, HALF),
        occ_energy, virt_energy)
    weight = -4.0 * gap / (gap * gap + freq_point * freq_point)

    plans = []
    for batch in BATCHES:
        used = sorted({WHERE[r][t[i:i + 2]] for r in range(4) for t in batch[r] for i in (0, 2)})
        table, held_most = batch_tables(batch, used)
        row = lax.dynamic_index_in_dim(jnp.asarray(table), role, axis=0, keepdims=False)
        row = jnp.concatenate([row, lax.dynamic_index_in_dim(jnp.asarray(ROW_ORDER), y, axis=0, keepdims=False)])
        plans.append([used, row, held_most])
    entries = lax.dynamic_index_in_dim(jnp.asarray(entry_table()), role * 2 + x_hi, axis=0, keepdims=False)
    rows = [plan[1] for plan in plans]
    halo_a, far_a, sib, scales, weight, entries, rows = lax.optimization_barrier(
        (halo_a, far_a, sib, scales, weight, entries, rows))

    far_b = aux_permute(after(other, far_a), [(1, 3, 0), (2, 0, 0)])
    halo_b = aux_permute(after(mine, halo_a), [(1, 1, -1), (2, 2, 1)])
    far_a_sib = aux_permute(far_a, [(1, 0, 0), (2, 3, 0)])
    halo_a_sib = aux_permute(halo_a, [(3, 2, 0)])
    minor = aux_permute(far_a, [(1, 0, 1), (2, 2, -1)])

    held = {OWN: mine, SIB: sib, FAR_A: far_a, HALO_A: halo_a}

    def tiles(number):
        used, _, held_most = plans[number]
        return tile_batch(BATCHES[number], rows[number], held_most, weight, [held[s] for s in used])

    def first_round(sends):
        return [y_permute(sends[0], 1), y_permute(sends[1], -1)]

    partial0 = tiles(0)
    sends0 = first_sends(partial0, scales)
    held[FAR_A_SIB], held[HALO_A_SIB] = after([far_a_sib, halo_a_sib], sends0)
    got0 = first_round(sends0)
    partial1 = tiles(1)
    sends1 = first_sends(partial1, scales)
    got0, sends1 = lax.optimization_barrier((got0, sends1))
    got1 = first_round(sends1)
    more = second_sends(partial0, got0, scales)
    far_b, halo_b, minor, got1, more = lax.optimization_barrier((far_b, halo_b, minor, got1, more))
    held[FAR_B], held[HALO_B], held[MINOR] = far_b, halo_b, minor
    held[FAR_B_SIB] = aux_permute(far_b, [(0, 1, 0), (3, 2, 0)])
    held[HALO_B_SIB] = aux_permute(halo_b, [(2, 3, 0)])
    more = [jnp.concatenate(pair) for pair in zip(more, second_sends(partial1, got1, scales))]
    more = first_round(more)
    partial2 = tiles(2)
    sends2 = first_sends(partial2, scales)
    got2 = first_round(sends2)
    more = after(more, sends2)
    more0, more1 = [m[:2] for m in more], [m[2:] for m in more]
    moved0 = [finish(partial0, got0, more0, scales, slice(1, 2)), finish(partial1, got1, more1, scales, slice(1, 2))]
    moved0 = narrow(jnp.concatenate([tile[h] for h in range(2) for tile in moved0]), scales)
    rows[3], moved0 = lax.optimization_barrier((rows[3], moved0, sends2))[:2]
    moved0 = aux_permute(moved0, [(0, 0, 1)])
    partial3 = tiles(3)
    sends3 = first_sends(partial3, scales)
    got2, moved0 = lax.optimization_barrier((got2, moved0, partial3))[:2]
    sends2 = second_sends(partial2, got2, scales)
    more2 = first_round(sends2)
    sends3 = after(sends3, sends2)
    got3 = first_round(sends3)
    more2 = after(more2, sends3)
    total2 = finish(partial2, got2, more2, scales)
    moved2 = narrow(jnp.concatenate(total2), scales)
    more0, more1 = after([more0, more1], moved2)
    total0 = finish(partial0, got0, more0, scales)
    total1 = finish(partial1, got1, more1, scales)
    moved2 = aux_permute(moved2, [(0, 0, 1), (1, 1, 1), (2, 2, 1)])
    got3, moved2 = lax.optimization_barrier((got3, moved2))
    more3 = both_ways(y_permute, *second_sends(partial3, got3, scales))
    moved0, moved2 = wide(moved0, scales), wide(moved2, scales)
    total3 = finish(partial3, got3, more3, scales)
    slots = jnp.concatenate(total0 + total1 + total2 + total3 + [moved0, moved2])
    terms = pick_parts(entries, slots).reshape(8, 2, PART, ROWS)
    got = both_ways(x_permute, *first_sends(terms, scales))
    zero, one = finish(terms, got, both_ways(x_permute, *second_sends(terms, got, scales)), scales)
    final = [zero[0], zero[1], one[0], one[1]]

    crossed = narrow(jnp.stack(final[1:]), scales).reshape(3, PART, 8, PART)
    crossed = lax.all_to_all(crossed, "pair", split_axis=2, concat_axis=1, tiled=True)
    crossed = crossed.reshape(3, ROWS, PART)

    swapped = aux_permute(after(narrow(one[0], scales), crossed), [(2, 3, 0), (3, 2, 0)])
    lower = [final[0], final[1], jnp.where(x_lo == 1, wide(swapped, scales), final[2]), final[3]]

    back = [
        [(0, 3, -1), (1, 0, 0), (2, 1, 0), (3, 2, 0)],
        [(0, 2, -1), (1, 3, -1), (2, 1, 0), (3, 0, 0)],
        [(0, 1, -1), (1, 2, -1), (2, 3, -1), (3, 0, 0)],
    ]
    upper = [wide(aux_permute(crossed[o], back[o]), scales).T for o in range(3)]
    return jnp.stack(lower[::-1] + upper)


def solution(mesh):
    return jax.shard_map(
        local,
        mesh=mesh,
        in_specs=(P("aux", "pair"), P("pair"), P("pair"), P(), P()),
        out_specs=P(None, ("aux", "pair"), None),
        check_vma=False,
    )
```

```python
import functools

import jax
import jax.numpy as jnp
import numpy as np
from jax import lax
from jax.experimental import pallas as pl
from jax.experimental.pallas import tpu as pltpu
from jax.sharding import PartitionSpec as P

ROWS = 768
HALF = 3072
PART = 96
PLANES = 4
WIDE = 256
freq_point = 0.5

OWN, SIB, FAR_A, FAR_A_SIB, FAR_B, FAR_B_SIB, HALO_A, HALO_B, HALO_A_SIB, HALO_B_SIB, MINOR = range(11)

WHERE = [
    {"A0": OWN, "A1": SIB, "A2": FAR_B, "A3": FAR_A_SIB, "P0": HALO_A, "B3": MINOR},
    {"A1": OWN, "A0": SIB, "A3": FAR_A, "A2": FAR_B_SIB, "P1": HALO_B},
    {"A2": OWN, "A3": SIB, "A0": FAR_A, "A1": FAR_B_SIB, "B2": HALO_B, "B3": HALO_A_SIB, "P0": MINOR},
    {"A3": OWN, "A2": SIB, "A1": FAR_B, "A0": FAR_A_SIB, "B3": HALO_A, "B2": HALO_B_SIB},
]

BATCHES = [
    [["A0A0", "P0A1"],
     ["A1A0", "A1A1"],
     ["A2A2", "A0A0"],
     ["A3A2", "A3A3"]],
    [["A3A1", "P0A3"],
     ["A3A0", "A3A3"],
     ["A0B3", "A2B3"],
     ["A3A0", "A2A0"]],
    [["P0A2", "A2A1"],
     ["P1A2", "P1A3"],
     ["P0A1", "A0B2"],
     ["A1A0", "A1A1"]],
    [["A2A2", "A2B3"],
     ["A3A2", "A2A0"],
     ["A2A1", "A3A1"],
     ["A1B3", "A1B2"]],
]
MOVED = [["A0B1", "A0B3", "A0B2", None], [None, None, "A1B2", "A1B3"],
         [None, None, "A0B1", None], [None, None, None, None]]
ENTRIES = [
    [["A0A0", "A0B3", "A0B2", "A0B1"], ["A2A2", "A2A1", "A3A1", "A2B3"]],
    [["A1A1", "A1A0", "A1B3", "A1B2"], ["A3A3", "A3A2", "A2A0", "A3A0"]],
]
ORDER = [(2, 0), (1, 1), (2, 1), (3, 0), (0, 0), (0, 1), (1, 0), (3, 1)]
ROW_ORDER = np.array([[ORDER.index(((rows % 4 - y) % 4, rows // 4)) for rows in range(8)] for y in range(4)], np.int32)


def batch_tables(batch, sources):
    held_most = 0
    plans = []
    for role, tiles in enumerate(batch):
        held = []
        first = []
        for step, tile in enumerate(tiles):
            for block in (tile[:2], tile[2:]):
                if block not in held:
                    held.append(block)
                    first.append(step)
        plans.append((held, first))
        held_most = max(held_most, len(held))
    rows = []
    for role, tiles in enumerate(batch):
        held, first = plans[role]
        left = [held.index(tile[:2]) for tile in tiles]
        right = [held.index(tile[2:]) for tile in tiles]
        fresh = [int(i == 0 or left[i] != left[i - 1]) for i in range(len(tiles))]
        pad = held_most - len(held)
        source = [sources.index(WHERE[role][block]) for block in held] + [-1] * pad
        rows.append(left + right + fresh + source + first + [-1] * pad)
    return np.array(rows, np.int32), held_most


def tiles_kernel(count, held_most, sources, table, weight, *refs):
    source_refs = refs[:sources]
    out, held, scaled, sems = refs[sources:]
    step = pl.program_id(0)
    source_at = 3 * count
    first_at = source_at + held_most

    def fetch(of_first):
        for j in range(held_most):
            for k in range(sources):
                @pl.when((table[source_at + j] == k) & ((table[first_at + j] == 0) == of_first))
                def _():
                    pltpu.make_async_copy(source_refs[k], held.at[j], sems.at[j]).start()

    @pl.when(step == 0)
    def _():
        fetch(True)

    def wait(block):
        for j in range(held_most):
            @pl.when((table[first_at + j] == step) & (block == j))
            def _():
                pltpu.make_async_copy(source_refs[0], held.at[j], sems.at[j]).wait()

    left = table[step]
    right = table[count + step]
    wait(left)

    @pl.when(table[2 * count + step] == 1)
    def _():
        @pl.loop(0, ROWS // 32)
        def _(i):
            rows = pl.ds(pl.multiple_of(i * 32, 32), 32)
            scaled[rows, :] = (held[left, rows, :].astype(jnp.float32) * weight[...]).astype(jnp.bfloat16)

    @pl.when(left != right)
    def _():
        wait(right)

    @pl.when(step == 0)
    def _():
        fetch(False)

    order_at = first_at + held_most
    for n in range(ROWS // WIDE):
        columns = slice(n * WIDE, (n + 1) * WIDE)
        acc = lax.dot_general(
            scaled[...], held[right, columns, :],
            (((1,), (1,)), ((), ())), preferred_element_type=jnp.float32)
        for rows in range(8):
            out[table[order_at + rows], 0, :, columns] = acc[rows * PART:(rows + 1) * PART]


def tile_batch(batch, table_row, held_most, weight, sources):
    count = len(batch[0])
    return pl.pallas_call(
        functools.partial(tiles_kernel, count, held_most, len(sources)),
        grid_spec=pltpu.PrefetchScalarGridSpec(
            num_scalar_prefetch=1,
            grid=(count,),
            in_specs=[pl.BlockSpec((1, HALF), lambda i, t: (0, 0))]
            + [pl.BlockSpec(memory_space=pl.ANY)] * len(sources),
            out_specs=pl.BlockSpec((8, 1, PART, ROWS), lambda i, t: (0, i, 0, 0)),
            scratch_shapes=[
                pltpu.VMEM((held_most, ROWS, HALF), jnp.bfloat16),
                pltpu.VMEM((ROWS, HALF), jnp.bfloat16),
                pltpu.SemaphoreType.DMA((held_most,)),
            ],
        ),
        out_shape=jax.ShapeDtypeStruct((8, count, PART, ROWS), jnp.float32),
        compiler_params=pltpu.CompilerParams(
            dimension_semantics=("arbitrary",), vmem_limit_bytes=(held_most + 2) * ROWS * HALF * 2 + 4 * 1024 * 1024),
        cost_estimate=pl.CostEstimate(
            flops=count * ROWS * ROWS,
            bytes_accessed=count * ROWS * ROWS,
            transcendentals=0),
    )(table_row, weight, *sources)


def lookup(table, index):
    blocks = table.shape[0]
    high = lax.shift_right_logical(index, 7)
    low = jnp.bitwise_and(index, 127)
    pairs = index.shape[1]
    hot = jnp.where(lax.broadcasted_iota(jnp.int32, (blocks, pairs), 0) == high, 1.0, 0.0).astype(jnp.bfloat16)
    rest = table
    column = jnp.zeros((128, pairs), jnp.float32)
    for _ in range(3):
        piece = rest.astype(jnp.bfloat16)
        rest = rest - piece.astype(jnp.float32)
        column = column + lax.dot_general(
            piece, hot, (((0,), (0,)), ((), ())), preferred_element_type=jnp.float32)
    mask = lax.broadcasted_iota(jnp.int32, (128, pairs), 0) == low
    return jnp.sum(jnp.where(mask, column, 0.0), axis=0, keepdims=True)


def gap_kernel(occ_index, virt_index, occ_energy, virt_energy, gap):
    gap[...] = lookup(virt_energy[...], virt_index[...]) - lookup(occ_energy[...], occ_index[...])


def pair_gaps(occ_index, virt_index, occ_energy, virt_energy):
    block = 512
    pairs = occ_index.shape[0]
    occ_table = occ_energy.reshape(-1, 128)
    virt_table = virt_energy.reshape(-1, 128)
    line = pl.BlockSpec((1, block), lambda i: (0, i))
    return pl.pallas_call(
        gap_kernel,
        grid=(pairs // block,),
        in_specs=[line, line,
                  pl.BlockSpec(occ_table.shape, lambda i: (0, 0)),
                  pl.BlockSpec(virt_table.shape, lambda i: (0, 0))],
        out_specs=line,
        out_shape=jax.ShapeDtypeStruct((1, pairs), jnp.float32),
        cost_estimate=pl.CostEstimate(flops=6 * 128 * 288 * pairs, bytes_accessed=200000, transcendentals=0),
    )(occ_index[None, :], virt_index[None, :], occ_table, virt_table)


def halves_kernel(x_lo, coeffs, mine, other, largest):
    for low in range(2):
        @pl.when(x_lo[0] == low)
        def _():
            mine[...] = coeffs[:, low * HALF:(low + 1) * HALF]
            other[...] = coeffs[:, (1 - low) * HALF:(2 - low) * HALF]

    @pl.when(pl.program_id(0) == 0)
    def _():
        largest[...] = jnp.zeros_like(largest)

    top = jnp.zeros((coeffs.shape[0], 128), jnp.float32)
    for c in range(coeffs.shape[1] // 128):
        top = jnp.maximum(top, jnp.abs(coeffs[:, c * 128:(c + 1) * 128].astype(jnp.float32)))
    largest[...] = jnp.maximum(largest[...], jnp.max(top.reshape(-1, 8, 128), axis=0))


def cut_in_halves(x_lo, coeffs):
    half = jax.ShapeDtypeStruct((ROWS, HALF), jnp.bfloat16)
    block = pl.BlockSpec((PART, HALF), lambda i, t: (i, 0))
    return pl.pallas_call(
        halves_kernel,
        grid_spec=pltpu.PrefetchScalarGridSpec(
            num_scalar_prefetch=1,
            grid=(ROWS // PART,),
            in_specs=[pl.BlockSpec((PART, 2 * HALF), lambda i, t: (i, 0))],
            out_specs=[block, block, pl.BlockSpec((8, 128), lambda i, t: (0, 0))],
        ),
        out_shape=[half, half, jax.ShapeDtypeStruct((8, 128), jnp.float32)],
        compiler_params=pltpu.CompilerParams(vmem_limit_bytes=12 * 1024 * 1024),
        cost_estimate=pl.CostEstimate(flops=0, bytes_accessed=PART * ROWS, transcendentals=0),
    )(x_lo[None], coeffs)


def moves(pairs):
    return [(z * 4 + src, (z + dz) % PLANES * 4 + dst) for z in range(PLANES) for src, dst, dz in pairs]


def aux_permute(value, pairs):
    return lax.ppermute(value, "aux", moves(pairs))


def y_permute(value, by):
    return lax.ppermute(value, "pair", [(h * 4 + y, h * 4 + (y + by) % 4) for h in range(2) for y in range(4)])


def x_permute(value, by, roles=range(4)):
    perm = []
    for z in range(PLANES):
        for x in range(4):
            to = (x + by) % 4
            for core in range(2):
                if x % 2 * 2 + core not in roles:
                    continue
                for y in range(4):
                    source = (z * 4 + x % 2 * 2 + core) * 8 + x // 2 * 4 + y
                    perm.append((source, (z * 4 + to % 2 * 2 + core) * 8 + to // 2 * 4 + y))
    return lax.ppermute(value, ("aux", "pair"), perm)


def both_ways(permute, up, down):
    return lax.optimization_barrier((permute(up, 1), permute(down, -1)))


def first_sends(terms, scales):
    return [narrow(terms[0:2], scales), narrow(terms[2:4], scales)]


def second_sends(terms, got, scales):
    return [narrow(terms[6] + wide(got[0][0], scales), scales),
            narrow(terms[7] + wide(got[1][0], scales), scales)]


def finish(terms, got, more, scales, slots=slice(None)):
    zero = terms[4][slots] + wide(got[1][1][slots], scales) + wide(more[0][slots], scales)
    one = terms[5][slots] + wide(got[0][1][slots], scales) + wide(more[1][slots], scales)
    return [zero, one]


def slot_names(role):
    names = []
    for batch in BATCHES:
        names += [(tile, h) for h in range(2) for tile in batch[role]]
    early, late = MOVED[role][:2], MOVED[role][2:]
    names += [(tile, h) for h in range(2) for tile in early]
    names += [(tile, h) for h in range(2) for tile in late]
    return names


def entry_table():
    rows = []
    for role in range(4):
        names = slot_names(role)
        for x_hi in range(2):
            row = []
            for k, d in ORDER:
                to = (x_hi * 2 + role // 2 + k) % 4
                row += [names.index((tile, to // 2)) for tile in ENTRIES[role % 2][to % 2][2 * d:2 * d + 2]]
            rows.append(row)
    return np.array(rows, np.int32)


def pick_kernel(table, slots, parts):
    for i in range(16):
        parts[i] = slots[table[i]]


def pick_parts(table, slots):
    return pl.pallas_call(
        pick_kernel,
        in_specs=[pl.BlockSpec(memory_space=pltpu.SMEM), pl.BlockSpec(memory_space=pltpu.VMEM)],
        out_specs=pl.BlockSpec(memory_space=pltpu.VMEM),
        out_shape=jax.ShapeDtypeStruct((16, PART, ROWS), jnp.float32),
        compiler_params=pltpu.CompilerParams(vmem_limit_bytes=16 * 1024 * 1024),
        cost_estimate=pl.CostEstimate(flops=0, bytes_accessed=PART * ROWS, transcendentals=0),
    )(table, slots)


def largest_round(value, permute):
    got = [permute(value, by) for by in (1, 2, 3)]
    return jnp.maximum(jnp.maximum(value, got[0]), jnp.maximum(got[1], got[2]))


def scales_of(largest):
    bound = 8.0 * HALF * 4 * largest * largest * 4.0
    scale = 32768.0 / jnp.maximum(bound, 1e-30)
    return scale, 1.0 / scale


def narrow(value, scales):
    return (value * scales[0]).astype(jnp.float16)


def wide(value, scales):
    return value.astype(jnp.float32) * scales[1]


def after(value, other):
    return lax.optimization_barrier((value, other))[0]


def local(coeffs, occ_index, virt_index, occ_energy, virt_energy):
    role = lax.rem(lax.axis_index("aux"), 4)
    x_lo = role // 2
    x_hi = lax.axis_index("pair") // 4
    y = lax.rem(lax.axis_index("pair"), 4)

    mine, other, largest = cut_in_halves(x_lo.astype(jnp.int32), coeffs)
    halo_a = aux_permute(mine, [(0, 0, -1), (3, 3, 1)])
    far_a = aux_permute(other, [(0, 2, 0), (3, 1, 0)])
    sib = aux_permute(mine, [(0, 1, 0), (1, 0, 0), (2, 3, 0), (3, 2, 0)])

    largest = jnp.maximum(largest, aux_permute(largest, [(0, 1, 0), (1, 0, 0), (2, 3, 0), (3, 2, 0)]))
    largest = largest_round(largest, y_permute)
    largest = jnp.maximum(largest, x_permute(largest, 2, (1, 2)))
    largest = jnp.maximum(largest, aux_permute(largest, [(1, 2, 0), (2, 1, 0)]))
    largest = jnp.maximum(largest, aux_permute(largest, [(1, 1, 2), (2, 2, 2)]))
    largest = jnp.maximum(largest, aux_permute(largest, [(1, 1, 1), (2, 2, 1)]))
    largest = jnp.maximum(largest, aux_permute(largest, [(1, 0, 0), (2, 3, 0)]))
    scales = scales_of(jnp.max(largest))

    occ_index, virt_index = after([occ_index, virt_index], mine)
    begin = x_lo * HALF
    gap = pair_gaps(
        lax.dynamic_slice_in_dim(occ_index, begin, HALF),
        lax.dynamic_slice_in_dim(virt_index, begin, HALF),
        occ_energy, virt_energy)
    weight = -4.0 * gap / (gap * gap + freq_point * freq_point)

    plans = []
    for batch in BATCHES:
        used = sorted({WHERE[r][t[i:i + 2]] for r in range(4) for t in batch[r] for i in (0, 2)})
        table, held_most = batch_tables(batch, used)
        row = lax.dynamic_index_in_dim(jnp.asarray(table), role, axis=0, keepdims=False)
        row = jnp.concatenate([row, lax.dynamic_index_in_dim(jnp.asarray(ROW_ORDER), y, axis=0, keepdims=False)])
        plans.append([used, row, held_most])
    entries = lax.dynamic_index_in_dim(jnp.asarray(entry_table()), role * 2 + x_hi, axis=0, keepdims=False)
    rows = [plan[1] for plan in plans]
    halo_a, far_a, sib, scales, weight, entries, rows = lax.optimization_barrier(
        (halo_a, far_a, sib, scales, weight, entries, rows))

    far_b = aux_permute(after(other, far_a), [(1, 3, 0), (2, 0, 0)])
    halo_b = aux_permute(after(mine, halo_a), [(1, 1, -1), (2, 2, 1)])
    far_a_sib = aux_permute(far_a, [(1, 0, 0), (2, 3, 0)])
    halo_a_sib = aux_permute(halo_a, [(3, 2, 0)])
    minor = aux_permute(far_a, [(1, 0, 1), (2, 2, -1)])

    held = {OWN: mine, SIB: sib, FAR_A: far_a, HALO_A: halo_a}

    def tiles(number):
        used, _, held_most = plans[number]
        return tile_batch(BATCHES[number], rows[number], held_most, weight, [held[s] for s in used])

    def first_round(sends):
        return [y_permute(sends[0], 1), y_permute(sends[1], -1)]

    partial0 = tiles(0)
    sends0 = first_sends(partial0, scales)
    held[FAR_A_SIB], held[HALO_A_SIB] = after([far_a_sib, halo_a_sib], sends0)
    got0 = first_round(sends0)
    partial1 = tiles(1)
    sends1 = first_sends(partial1, scales)
    got0, sends1 = lax.optimization_barrier((got0, sends1))
    got1 = first_round(sends1)
    more = second_sends(partial0, got0, scales)
    far_b, halo_b, minor, got1, more = lax.optimization_barrier((far_b, halo_b, minor, got1, more))
    held[FAR_B], held[HALO_B], held[MINOR] = far_b, halo_b, minor
    held[FAR_B_SIB] = aux_permute(far_b, [(0, 1, 0), (3, 2, 0)])
    held[HALO_B_SIB] = aux_permute(halo_b, [(2, 3, 0)])
    more = [jnp.concatenate(pair) for pair in zip(more, second_sends(partial1, got1, scales))]
    more = first_round(more)
    partial2 = tiles(2)
    sends2 = first_sends(partial2, scales)
    got2 = first_round(sends2)
    more = after(more, sends2)
    more0, more1 = [m[:2] for m in more], [m[2:] for m in more]
    moved0 = [finish(partial0, got0, more0, scales, slice(1, 2)), finish(partial1, got1, more1, scales, slice(1, 2))]
    moved0 = narrow(jnp.concatenate([tile[h] for h in range(2) for tile in moved0]), scales)
    rows[3], moved0 = lax.optimization_barrier((rows[3], moved0, sends2))[:2]
    moved0 = aux_permute(moved0, [(0, 0, 1)])
    partial3 = tiles(3)
    sends3 = first_sends(partial3, scales)
    got2, moved0 = lax.optimization_barrier((got2, moved0, partial3))[:2]
    sends2 = second_sends(partial2, got2, scales)
    more2 = first_round(sends2)
    sends3 = after(sends3, sends2)
    got3 = first_round(sends3)
    more2 = after(more2, sends3)
    total2 = finish(partial2, got2, more2, scales)
    moved2 = narrow(jnp.concatenate(total2), scales)
    more0, more1 = after([more0, more1], moved2)
    total0 = finish(partial0, got0, more0, scales)
    total1 = finish(partial1, got1, more1, scales)
    moved2 = aux_permute(moved2, [(0, 0, 1), (1, 1, 1), (2, 2, 1)])
    got3, moved2 = lax.optimization_barrier((got3, moved2))
    more3 = both_ways(y_permute, *second_sends(partial3, got3, scales))
    moved0, moved2 = wide(moved0, scales), wide(moved2, scales)
    total3 = finish(partial3, got3, more3, scales)
    slots = jnp.concatenate(total0 + total1 + total2 + total3 + [moved0, moved2])
    terms = pick_parts(entries, slots).reshape(8, 2, PART, ROWS)
    got = both_ways(x_permute, *first_sends(terms, scales))
    zero, one = finish(terms, got, both_ways(x_permute, *second_sends(terms, got, scales)), scales)
    final = [zero[0], zero[1], one[0], one[1]]

    crossed = narrow(jnp.stack(final[1:]), scales).reshape(3, PART, 8, PART)
    crossed = lax.all_to_all(crossed, "pair", split_axis=2, concat_axis=1, tiled=True)
    crossed = crossed.reshape(3, ROWS, PART)

    swapped = aux_permute(after(narrow(one[0], scales), crossed), [(2, 3, 0), (3, 2, 0)])
    lower = [final[0], final[1], jnp.where(x_lo == 1, wide(swapped, scales), final[2]), final[3]]

    back = [
        [(0, 3, -1), (1, 0, 0), (2, 1, 0), (3, 2, 0)],
        [(0, 2, -1), (1, 3, -1), (2, 1, 0), (3, 0, 0)],
        [(0, 1, -1), (1, 2, -1), (2, 3, -1), (3, 0, 0)],
    ]
    upper = [wide(aux_permute(crossed[o], back[o]), scales).T for o in range(3)]
    return jnp.stack(lower[::-1] + upper)


def solution(mesh):
    return jax.shard_map(
        local,
        mesh=mesh,
        in_specs=(P("aux", "pair"), P("pair"), P("pair"), P(), P()),
        out_specs=P(None, ("aux", "pair"), None),
        check_vma=False,
    )
```

```python
import functools

import jax
import jax.numpy as jnp
import numpy as np
from jax import lax
from jax.experimental import pallas as pl
from jax.experimental.pallas import tpu as pltpu
from jax.sharding import PartitionSpec as P

ROWS = 768
HALF = 3072
PART = 96
PLANES = 4
WIDE = 256
freq_point = 0.5

OWN, SIB, FAR_A, FAR_A_SIB, FAR_B, FAR_B_SIB, HALO_A, HALO_B, HALO_A_SIB, HALO_B_SIB, MINOR = range(11)

WHERE = [
    {"A0": OWN, "A1": SIB, "A2": FAR_B, "A3": FAR_A_SIB, "P0": HALO_A, "B3": MINOR},
    {"A1": OWN, "A0": SIB, "A3": FAR_A, "A2": FAR_B_SIB, "P1": HALO_B},
    {"A2": OWN, "A3": SIB, "A0": FAR_A, "A1": FAR_B_SIB, "B2": HALO_B, "B3": HALO_A_SIB, "P0": MINOR},
    {"A3": OWN, "A2": SIB, "A1": FAR_B, "A0": FAR_A_SIB, "B3": HALO_A, "B2": HALO_B_SIB},
]

BATCHES = [
    [["A0A0", "P0A1"],
     ["A1A0", "A1A1"],
     ["A2A2", "A0A0"],
     ["A3A2", "A3A3"]],
    [["A3A1", "P0A3"],
     ["A3A0", "A3A3"],
     ["A0B3", "A2B3"],
     ["A3A0", "A2A0"]],
    [["P0A2", "A2A1"],
     ["P1A2", "P1A3"],
     ["P0A1", "A0B2"],
     ["A1A0", "A1A1"]],
    [["A2A2", "A2B3"],
     ["A3A2", "A2A0"],
     ["A2A1", "A3A1"],
     ["A1B3", "A1B2"]],
]
MOVED = [["A0B1", "A0B3", "A0B2", None], [None, None, "A1B2", "A1B3"],
         [None, None, "A0B1", None], [None, None, None, None]]
ENTRIES = [
    [["A0A0", "A0B3", "A0B2", "A0B1"], ["A2A2", "A2A1", "A3A1", "A2B3"]],
    [["A1A1", "A1A0", "A1B3", "A1B2"], ["A3A3", "A3A2", "A2A0", "A3A0"]],
]
ORDER = [(2, 0), (1, 1), (2, 1), (3, 0), (0, 0), (0, 1), (1, 0), (3, 1)]
ROW_ORDER = np.array([[ORDER.index(((rows % 4 - y) % 4, rows // 4)) for rows in range(8)] for y in range(4)], np.int32)


def batch_tables(batch, sources):
    held_most = 0
    plans = []
    for role, tiles in enumerate(batch):
        held = []
        first = []
        for step, tile in enumerate(tiles):
            for block in (tile[:2], tile[2:]):
                if block not in held:
                    held.append(block)
                    first.append(step)
        plans.append((held, first))
        held_most = max(held_most, len(held))
    rows = []
    for role, tiles in enumerate(batch):
        held, first = plans[role]
        left = [held.index(tile[:2]) for tile in tiles]
        right = [held.index(tile[2:]) for tile in tiles]
        fresh = [int(i == 0 or left[i] != left[i - 1]) for i in range(len(tiles))]
        pad = held_most - len(held)
        source = [sources.index(WHERE[role][block]) for block in held] + [-1] * pad
        rows.append(left + right + fresh + source + first + [-1] * pad)
    return np.array(rows, np.int32), held_most


def tiles_kernel(count, held_most, sources, table, weight, *refs):
    source_refs = refs[:sources]
    out, held, scaled, sems = refs[sources:]
    step = pl.program_id(0)
    source_at = 3 * count
    first_at = source_at + held_most

    def fetch(of_first):
        for j in range(held_most):
            for k in range(sources):
                @pl.when((table[source_at + j] == k) & ((table[first_at + j] == 0) == of_first))
                def _():
                    pltpu.make_async_copy(source_refs[k], held.at[j], sems.at[j]).start()

    @pl.when(step == 0)
    def _():
        fetch(True)

    def wait(block):
        for j in range(held_most):
            @pl.when((table[first_at + j] == step) & (block == j))
            def _():
                pltpu.make_async_copy(source_refs[0], held.at[j], sems.at[j]).wait()

    left = table[step]
    right = table[count + step]
    wait(left)

    @pl.when(table[2 * count + step] == 1)
    def _():
        @pl.loop(0, ROWS // 32)
        def _(i):
            rows = pl.ds(pl.multiple_of(i * 32, 32), 32)
            scaled[rows, :] = (held[left, rows, :].astype(jnp.float32) * weight[...]).astype(jnp.bfloat16)

    @pl.when(left != right)
    def _():
        wait(right)

    @pl.when(step == 0)
    def _():
        fetch(False)

    order_at = first_at + held_most
    for n in range(ROWS // WIDE):
        columns = slice(n * WIDE, (n + 1) * WIDE)
        acc = lax.dot_general(
            scaled[...], held[right, columns, :],
            (((1,), (1,)), ((), ())), preferred_element_type=jnp.float32)
        for rows in range(8):
            out[table[order_at + rows], 0, :, columns] = acc[rows * PART:(rows + 1) * PART]


def tile_batch(batch, table_row, held_most, weight, sources):
    count = len(batch[0])
    return pl.pallas_call(
        functools.partial(tiles_kernel, count, held_most, len(sources)),
        grid_spec=pltpu.PrefetchScalarGridSpec(
            num_scalar_prefetch=1,
            grid=(count,),
            in_specs=[pl.BlockSpec((1, HALF), lambda i, t: (0, 0))]
            + [pl.BlockSpec(memory_space=pl.ANY)] * len(sources),
            out_specs=pl.BlockSpec((8, 1, PART, ROWS), lambda i, t: (0, i, 0, 0)),
            scratch_shapes=[
                pltpu.VMEM((held_most, ROWS, HALF), jnp.bfloat16),
                pltpu.VMEM((ROWS, HALF), jnp.bfloat16),
                pltpu.SemaphoreType.DMA((held_most,)),
            ],
        ),
        out_shape=jax.ShapeDtypeStruct((8, count, PART, ROWS), jnp.float32),
        compiler_params=pltpu.CompilerParams(
            dimension_semantics=("arbitrary",), vmem_limit_bytes=36 * 1024 * 1024),
        cost_estimate=pl.CostEstimate(
            flops=count * ROWS * ROWS,
            bytes_accessed=count * ROWS * ROWS,
            transcendentals=0),
    )(table_row, weight, *sources)


def lookup(table, index):
    blocks = table.shape[0]
    high = lax.shift_right_logical(index, 7)
    low = jnp.bitwise_and(index, 127)
    pairs = index.shape[1]
    hot = jnp.where(lax.broadcasted_iota(jnp.int32, (blocks, pairs), 0) == high, 1.0, 0.0).astype(jnp.bfloat16)
    rest = table
    column = jnp.zeros((128, pairs), jnp.float32)
    for _ in range(3):
        piece = rest.astype(jnp.bfloat16)
        rest = rest - piece.astype(jnp.float32)
        column = column + lax.dot_general(
            piece, hot, (((0,), (0,)), ((), ())), preferred_element_type=jnp.float32)
    mask = lax.broadcasted_iota(jnp.int32, (128, pairs), 0) == low
    return jnp.sum(jnp.where(mask, column, 0.0), axis=0, keepdims=True)


def gap_kernel(occ_index, virt_index, occ_energy, virt_energy, gap):
    gap[...] = lookup(virt_energy[...], virt_index[...]) - lookup(occ_energy[...], occ_index[...])


def pair_gaps(occ_index, virt_index, occ_energy, virt_energy):
    block = 512
    pairs = occ_index.shape[0]
    occ_table = occ_energy.reshape(-1, 128)
    virt_table = virt_energy.reshape(-1, 128)
    line = pl.BlockSpec((1, block), lambda i: (0, i))
    return pl.pallas_call(
        gap_kernel,
        grid=(pairs // block,),
        in_specs=[line, line,
                  pl.BlockSpec(occ_table.shape, lambda i: (0, 0)),
                  pl.BlockSpec(virt_table.shape, lambda i: (0, 0))],
        out_specs=line,
        out_shape=jax.ShapeDtypeStruct((1, pairs), jnp.float32),
        cost_estimate=pl.CostEstimate(flops=6 * 128 * 288 * pairs, bytes_accessed=200000, transcendentals=0),
    )(occ_index[None, :], virt_index[None, :], occ_table, virt_table)


def halves_kernel(x_lo, coeffs, mine, other, largest):
    for low in range(2):
        @pl.when(x_lo[0] == low)
        def _():
            mine[...] = coeffs[:, low * HALF:(low + 1) * HALF]
            other[...] = coeffs[:, (1 - low) * HALF:(2 - low) * HALF]

    @pl.when(pl.program_id(0) == 0)
    def _():
        largest[...] = jnp.zeros_like(largest)

    top = jnp.zeros((coeffs.shape[0], 128), jnp.float32)
    for c in range(coeffs.shape[1] // 128):
        top = jnp.maximum(top, jnp.abs(coeffs[:, c * 128:(c + 1) * 128].astype(jnp.float32)))
    largest[...] = jnp.maximum(largest[...], jnp.max(top.reshape(-1, 8, 128), axis=0))


def cut_in_halves(x_lo, coeffs):
    half = jax.ShapeDtypeStruct((ROWS, HALF), jnp.bfloat16)
    block = pl.BlockSpec((PART, HALF), lambda i, t: (i, 0))
    return pl.pallas_call(
        halves_kernel,
        grid_spec=pltpu.PrefetchScalarGridSpec(
            num_scalar_prefetch=1,
            grid=(ROWS // PART,),
            in_specs=[pl.BlockSpec((PART, 2 * HALF), lambda i, t: (i, 0))],
            out_specs=[block, block, pl.BlockSpec((8, 128), lambda i, t: (0, 0))],
        ),
        out_shape=[half, half, jax.ShapeDtypeStruct((8, 128), jnp.float32)],
        compiler_params=pltpu.CompilerParams(vmem_limit_bytes=24 * 1024 * 1024),
        cost_estimate=pl.CostEstimate(flops=0, bytes_accessed=PART * ROWS, transcendentals=0),
    )(x_lo[None], coeffs)


def moves(pairs):
    return [(z * 4 + src, (z + dz) % PLANES * 4 + dst) for z in range(PLANES) for src, dst, dz in pairs]


def aux_permute(value, pairs):
    return lax.ppermute(value, "aux", moves(pairs))


def y_permute(value, by):
    return lax.ppermute(value, "pair", [(h * 4 + y, h * 4 + (y + by) % 4) for h in range(2) for y in range(4)])


def x_permute(value, by, roles=range(4)):
    perm = []
    for z in range(PLANES):
        for x in range(4):
            to = (x + by) % 4
            for core in range(2):
                if x % 2 * 2 + core not in roles:
                    continue
                for y in range(4):
                    source = (z * 4 + x % 2 * 2 + core) * 8 + x // 2 * 4 + y
                    perm.append((source, (z * 4 + to % 2 * 2 + core) * 8 + to // 2 * 4 + y))
    return lax.ppermute(value, ("aux", "pair"), perm)


def both_ways(permute, up, down):
    return lax.optimization_barrier((permute(up, 1), permute(down, -1)))


def first_sends(terms, scales):
    return [narrow(terms[0:2], scales), narrow(terms[2:4], scales)]


def second_sends(terms, got, scales):
    return [narrow(terms[6] + wide(got[0][0], scales), scales),
            narrow(terms[7] + wide(got[1][0], scales), scales)]


def finish(terms, got, more, scales, slots=slice(None)):
    zero = terms[4][slots] + wide(got[1][1][slots], scales) + wide(more[0][slots], scales)
    one = terms[5][slots] + wide(got[0][1][slots], scales) + wide(more[1][slots], scales)
    return [zero, one]


def slot_names(role):
    names = []
    for batch in BATCHES:
        names += [(tile, h) for h in range(2) for tile in batch[role]]
    early, late = MOVED[role][:2], MOVED[role][2:]
    names += [(tile, h) for h in range(2) for tile in early]
    names += [(tile, h) for tile in late for h in range(2)]
    return names


def entry_table():
    rows = []
    for role in range(4):
        names = slot_names(role)
        for x_hi in range(2):
            row = []
            for k, d in ORDER:
                to = (x_hi * 2 + role // 2 + k) % 4
                row += [names.index((tile, to // 2)) for tile in ENTRIES[role % 2][to % 2][2 * d:2 * d + 2]]
            rows.append(row)
    return np.array(rows, np.int32)


def pick_kernel(table, slots, parts):
    for i in range(16):
        parts[i] = slots[table[i]]


def pick_parts(table, slots):
    return pl.pallas_call(
        pick_kernel,
        in_specs=[pl.BlockSpec(memory_space=pltpu.SMEM), pl.BlockSpec(memory_space=pltpu.VMEM)],
        out_specs=pl.BlockSpec(memory_space=pltpu.VMEM),
        out_shape=jax.ShapeDtypeStruct((16, PART, ROWS), jnp.float32),
        compiler_params=pltpu.CompilerParams(vmem_limit_bytes=20 * 1024 * 1024),
        cost_estimate=pl.CostEstimate(flops=0, bytes_accessed=PART * ROWS, transcendentals=0),
    )(table, slots)


def largest_round(value, permute):
    got = [permute(value, by) for by in (1, 2, 3)]
    return jnp.maximum(jnp.maximum(value, got[0]), jnp.maximum(got[1], got[2]))


def scales_of(largest):
    bound = 8.0 * HALF * 4 * largest * largest * 4.0
    scale = 32768.0 / jnp.maximum(bound, 1e-30)
    return scale, 1.0 / scale


def narrow(value, scales):
    return (value * scales[0]).astype(jnp.float16)


def wide(value, scales):
    return value.astype(jnp.float32) * scales[1]


def after(value, other):
    return lax.optimization_barrier((value, other))[0]


def local(coeffs, occ_index, virt_index, occ_energy, virt_energy):
    role = lax.rem(lax.axis_index("aux"), 4)
    x_lo = role // 2
    x_hi = lax.axis_index("pair") // 4
    y = lax.rem(lax.axis_index("pair"), 4)

    mine, other, largest = cut_in_halves(x_lo.astype(jnp.int32), coeffs)
    halo_a = aux_permute(mine, [(0, 0, -1), (3, 3, 1)])
    far_a = aux_permute(other, [(0, 2, 0), (3, 1, 0)])
    sib = aux_permute(mine, [(0, 1, 0), (1, 0, 0), (2, 3, 0), (3, 2, 0)])

    largest = jnp.maximum(largest, aux_permute(largest, [(0, 1, 0), (1, 0, 0), (2, 3, 0), (3, 2, 0)]))
    largest = largest_round(largest, y_permute)
    largest = jnp.maximum(largest, x_permute(largest, 2, (1, 2)))
    largest = jnp.maximum(largest, aux_permute(largest, [(1, 2, 0), (2, 1, 0)]))
    largest = jnp.maximum(largest, aux_permute(largest, [(1, 1, 2), (2, 2, 2)]))
    largest = jnp.maximum(largest, aux_permute(largest, [(1, 1, 1), (2, 2, 1)]))
    largest = jnp.maximum(largest, aux_permute(largest, [(1, 0, 0), (2, 3, 0)]))
    scales = scales_of(jnp.max(largest))

    occ_index, virt_index = after([occ_index, virt_index], mine)
    begin = x_lo * HALF
    gap = pair_gaps(
        lax.dynamic_slice_in_dim(occ_index, begin, HALF),
        lax.dynamic_slice_in_dim(virt_index, begin, HALF),
        occ_energy, virt_energy)
    weight = -4.0 * gap / (gap * gap + freq_point * freq_point)

    plans = []
    for batch in BATCHES:
        used = sorted({WHERE[r][t[i:i + 2]] for r in range(4) for t in batch[r] for i in (0, 2)})
        table, held_most = batch_tables(batch, used)
        row = lax.dynamic_index_in_dim(jnp.asarray(table), role, axis=0, keepdims=False)
        row = jnp.concatenate([row, lax.dynamic_index_in_dim(jnp.asarray(ROW_ORDER), y, axis=0, keepdims=False)])
        plans.append([used, row, held_most])
    entries = lax.dynamic_index_in_dim(jnp.asarray(entry_table()), role * 2 + x_hi, axis=0, keepdims=False)
    rows = [plan[1] for plan in plans]
    halo_a, far_a, sib, scales, weight, entries, rows = lax.optimization_barrier(
        (halo_a, far_a, sib, scales, weight, entries, rows))

    far_b = aux_permute(after(other, far_a), [(1, 3, 0), (2, 0, 0)])
    halo_b = aux_permute(after(mine, halo_a), [(1, 1, -1), (2, 2, 1)])
    far_a_sib = aux_permute(far_a, [(1, 0, 0), (2, 3, 0)])
    halo_a_sib = aux_permute(halo_a, [(3, 2, 0)])
    minor = aux_permute(far_a, [(1, 0, 1), (2, 2, -1)])

    held = {OWN: mine, SIB: sib, FAR_A: far_a, HALO_A: halo_a}

    def tiles(number):
        used, _, held_most = plans[number]
        return tile_batch(BATCHES[number], rows[number], held_most, weight, [held[s] for s in used])

    def first_round(sends):
        return [y_permute(sends[0], 1), y_permute(sends[1], -1)]

    partial0 = tiles(0)
    sends0 = first_sends(partial0, scales)
    held[FAR_A_SIB], held[HALO_A_SIB] = after([far_a_sib, halo_a_sib], sends0)
    got0 = first_round(sends0)
    partial1 = tiles(1)
    sends1 = first_sends(partial1, scales)
    got0, sends1 = lax.optimization_barrier((got0, sends1))
    got1 = first_round(sends1)
    more = second_sends(partial0, got0, scales)
    far_b, halo_b, minor, got1, more = lax.optimization_barrier((far_b, halo_b, minor, got1, more))
    held[FAR_B], held[HALO_B], held[MINOR] = far_b, halo_b, minor
    held[FAR_B_SIB] = aux_permute(far_b, [(0, 1, 0), (3, 2, 0)])
    held[HALO_B_SIB] = aux_permute(halo_b, [(2, 3, 0)])
    more = [jnp.concatenate(pair) for pair in zip(more, second_sends(partial1, got1, scales))]
    more = first_round(more)
    partial2 = tiles(2)
    sends2 = first_sends(partial2, scales)
    got2 = first_round(sends2)
    more = after(more, sends2)
    more0, more1 = [m[:2] for m in more], [m[2:] for m in more]
    moved0 = [finish(partial0, got0, more0, scales, slice(1, 2)), finish(partial1, got1, more1, scales, slice(1, 2))]
    moved0 = narrow(jnp.concatenate([tile[h] for h in range(2) for tile in moved0]), scales)
    rows[3], moved0 = lax.optimization_barrier((rows[3], moved0, sends2))[:2]
    moved0 = aux_permute(moved0, [(0, 0, 1)])
    partial3 = tiles(3)
    sends3 = first_sends(partial3, scales)
    got2, moved0 = lax.optimization_barrier((got2, moved0, partial3))[:2]
    sends2 = second_sends(partial2, got2, scales)
    more2 = first_round(sends2)
    sends3 = after(sends3, sends2)
    got3 = first_round(sends3)
    more2 = after(more2, sends3)
    total2 = finish(partial2, got2, more2, scales)
    moved2 = [narrow(jnp.stack([total2[0][i], total2[1][i]]), scales) for i in range(2)]
    more0, more1 = after([more0, more1], moved2)
    total0 = finish(partial0, got0, more0, scales)
    total1 = finish(partial1, got1, more1, scales)
    moved2 = [aux_permute(moved2[0], [(0, 0, 1), (1, 1, 1), (2, 2, 1)]), aux_permute(moved2[1], [(1, 1, 1)])]
    got3, moved2 = lax.optimization_barrier((got3, moved2))
    more3 = both_ways(y_permute, *second_sends(partial3, got3, scales))
    moved0, moved2 = wide(moved0, scales), wide(jnp.concatenate(moved2), scales)
    total3 = finish(partial3, got3, more3, scales)
    slots = jnp.concatenate(total0 + total1 + total2 + total3 + [moved0, moved2])
    terms = pick_parts(entries, slots).reshape(8, 2, PART, ROWS)
    got = both_ways(x_permute, *first_sends(terms, scales))
    zero, one = finish(terms, got, both_ways(x_permute, *second_sends(terms, got, scales)), scales)
    final = [zero[0], zero[1], one[0], one[1]]

    crossed = narrow(jnp.stack(final[1:]), scales).reshape(3, PART, 8, PART)
    crossed = lax.all_to_all(crossed, "pair", split_axis=2, concat_axis=1, tiled=True)
    crossed = crossed.reshape(3, ROWS, PART)

    swapped = aux_permute(after(narrow(one[0], scales), crossed), [(2, 3, 0), (3, 2, 0)])
    lower = [final[0], final[1], jnp.where(x_lo == 1, wide(swapped, scales), final[2]), final[3]]

    back = [
        [(0, 3, -1), (1, 0, 0), (2, 1, 0), (3, 2, 0)],
        [(0, 2, -1), (1, 3, -1), (2, 1, 0), (3, 0, 0)],
        [(0, 1, -1), (1, 2, -1), (2, 3, -1), (3, 0, 0)],
    ]
    upper = [wide(aux_permute(crossed[o], back[o]), scales).T for o in range(3)]
    return jnp.stack(lower[::-1] + upper)


def solution(mesh):
    return jax.shard_map(
        local,
        mesh=mesh,
        in_specs=(P("aux", "pair"), P("pair"), P("pair"), P(), P()),
        out_specs=P(None, ("aux", "pair"), None),
        check_vma=False,
    )
```

```python
import functools

import jax
import jax.numpy as jnp
import numpy as np
from jax import lax
from jax.experimental import pallas as pl
from jax.experimental.pallas import tpu as pltpu
from jax.sharding import PartitionSpec as P

ROWS = 768
HALF = 3072
PART = 96
PLANES = 4
WIDE = 768
freq_point = 0.5

OWN, SIB, FAR_A, FAR_A_SIB, FAR_B, FAR_B_SIB, HALO_A, HALO_B, HALO_A_SIB, HALO_B_SIB, MINOR = range(11)

WHERE = [
    {"A0": OWN, "A1": SIB, "A2": FAR_B, "A3": FAR_A_SIB, "P0": HALO_A, "B3": MINOR},
    {"A1": OWN, "A0": SIB, "A3": FAR_A, "A2": FAR_B_SIB, "P1": HALO_B},
    {"A2": OWN, "A3": SIB, "A0": FAR_A, "A1": FAR_B_SIB, "B2": HALO_B, "B3": HALO_A_SIB, "P0": MINOR},
    {"A3": OWN, "A2": SIB, "A1": FAR_B, "A0": FAR_A_SIB, "B3": HALO_A, "B2": HALO_B_SIB},
]

BATCHES = [
    [["A0A0", "P0A1"],
     ["A1A0", "A1A1"],
     ["A2A2", "A0A0"],
     ["A3A2", "A3A3"]],
    [["A3A1", "P0A3"],
     ["A3A0", "A3A3"],
     ["A0B3", "A2B3"],
     ["A3A0", "A2A0"]],
    [["P0A2", "A2A1"],
     ["P1A2", "P1A3"],
     ["P0A1", "A0B2"],
     ["A1A0", "A1A1"]],
    [["A2A2", "A2B3"],
     ["A3A2", "A2A0"],
     ["A2A1", "A3A1"],
     ["A1B3", "A1B2"]],
]
MOVED = [["A0B1", "A0B3", "A0B2", None], [None, None, "A1B2", "A1B3"],
         [None, None, "A0B1", None], [None, None, None, None]]
ENTRIES = [
    [["A0A0", "A0B3", "A0B2", "A0B1"], ["A2A2", "A2A1", "A3A1", "A2B3"]],
    [["A1A1", "A1A0", "A1B3", "A1B2"], ["A3A3", "A3A2", "A2A0", "A3A0"]],
]
ORDER = [(2, 0), (1, 1), (2, 1), (3, 0), (0, 0), (0, 1), (1, 0), (3, 1)]
ROW_ORDER = np.array([[ORDER.index(((rows % 4 - y) % 4, rows // 4)) for rows in range(8)] for y in range(4)], np.int32)


def batch_tables(batch, sources):
    held_most = 0
    plans = []
    for role, tiles in enumerate(batch):
        held = []
        first = []
        for step, tile in enumerate(tiles):
            for block in (tile[:2], tile[2:]):
                if block not in held:
                    held.append(block)
                    first.append(step)
        plans.append((held, first))
        held_most = max(held_most, len(held))
    rows = []
    for role, tiles in enumerate(batch):
        held, first = plans[role]
        left = [held.index(tile[:2]) for tile in tiles]
        right = [held.index(tile[2:]) for tile in tiles]
        fresh = [int(i == 0 or left[i] != left[i - 1]) for i in range(len(tiles))]
        pad = held_most - len(held)
        source = [sources.index(WHERE[role][block]) for block in held] + [-1] * pad
        rows.append(left + right + fresh + source + first + [-1] * pad)
    return np.array(rows, np.int32), held_most


def tiles_kernel(count, held_most, sources, table, weight, *refs):
    source_refs = refs[:sources]
    out, held, scaled, sems = refs[sources:]
    step = pl.program_id(0)
    source_at = 3 * count
    first_at = source_at + held_most

    def fetch(of_first):
        for j in range(held_most):
            for k in range(sources):
                @pl.when((table[source_at + j] == k) & ((table[first_at + j] == 0) == of_first))
                def _():
                    pltpu.make_async_copy(source_refs[k], held.at[j], sems.at[j]).start()

    @pl.when(step == 0)
    def _():
        fetch(True)

    def wait(block):
        for j in range(held_most):
            @pl.when((table[first_at + j] == step) & (block == j))
            def _():
                pltpu.make_async_copy(source_refs[0], held.at[j], sems.at[j]).wait()

    left = table[step]
    right = table[count + step]
    wait(left)

    @pl.when(table[2 * count + step] == 1)
    def _():
        @pl.loop(0, ROWS // 32)
        def _(i):
            rows = pl.ds(pl.multiple_of(i * 32, 32), 32)
            scaled[rows, :] = (held[left, rows, :].astype(jnp.float32) * weight[...]).astype(jnp.bfloat16)

    @pl.when(left != right)
    def _():
        wait(right)

    @pl.when(step == 0)
    def _():
        fetch(False)

    order_at = first_at + held_most
    for n in range(ROWS // WIDE):
        columns = slice(n * WIDE, (n + 1) * WIDE)
        acc = lax.dot_general(
            scaled[...], held[right, columns, :],
            (((1,), (1,)), ((), ())), preferred_element_type=jnp.float32)
        for rows in range(8):
            out[table[order_at + rows], 0, :, columns] = acc[rows * PART:(rows + 1) * PART]


def tile_batch(batch, table_row, held_most, weight, sources):
    count = len(batch[0])
    return pl.pallas_call(
        functools.partial(tiles_kernel, count, held_most, len(sources)),
        grid_spec=pltpu.PrefetchScalarGridSpec(
            num_scalar_prefetch=1,
            grid=(count,),
            in_specs=[pl.BlockSpec((1, HALF), lambda i, t: (0, 0))]
            + [pl.BlockSpec(memory_space=pl.ANY)] * len(sources),
            out_specs=pl.BlockSpec((8, 1, PART, ROWS), lambda i, t: (0, i, 0, 0)),
            scratch_shapes=[
                pltpu.VMEM((held_most, ROWS, HALF), jnp.bfloat16),
                pltpu.VMEM((ROWS, HALF), jnp.bfloat16),
                pltpu.SemaphoreType.DMA((held_most,)),
            ],
        ),
        out_shape=jax.ShapeDtypeStruct((8, count, PART, ROWS), jnp.float32),
        compiler_params=pltpu.CompilerParams(
            dimension_semantics=("arbitrary",), vmem_limit_bytes=36 * 1024 * 1024),
        cost_estimate=pl.CostEstimate(
            flops=count * ROWS * ROWS,
            bytes_accessed=count * ROWS * ROWS,
            transcendentals=0),
    )(table_row, weight, *sources)


def lookup(table, index):
    blocks = table.shape[0]
    high = lax.shift_right_logical(index, 7)
    low = jnp.bitwise_and(index, 127)
    pairs = index.shape[1]
    hot = jnp.where(lax.broadcasted_iota(jnp.int32, (blocks, pairs), 0) == high, 1.0, 0.0).astype(jnp.bfloat16)
    rest = table
    column = jnp.zeros((128, pairs), jnp.float32)
    for _ in range(3):
        piece = rest.astype(jnp.bfloat16)
        rest = rest - piece.astype(jnp.float32)
        column = column + lax.dot_general(
            piece, hot, (((0,), (0,)), ((), ())), preferred_element_type=jnp.float32)
    mask = lax.broadcasted_iota(jnp.int32, (128, pairs), 0) == low
    return jnp.sum(jnp.where(mask, column, 0.0), axis=0, keepdims=True)


def gap_kernel(occ_index, virt_index, occ_energy, virt_energy, gap):
    gap[...] = lookup(virt_energy[...], virt_index[...]) - lookup(occ_energy[...], occ_index[...])


def pair_gaps(occ_index, virt_index, occ_energy, virt_energy):
    block = 512
    pairs = occ_index.shape[0]
    occ_table = occ_energy.reshape(-1, 128)
    virt_table = virt_energy.reshape(-1, 128)
    line = pl.BlockSpec((1, block), lambda i: (0, i))
    return pl.pallas_call(
        gap_kernel,
        grid=(pairs // block,),
        in_specs=[line, line,
                  pl.BlockSpec(occ_table.shape, lambda i: (0, 0)),
                  pl.BlockSpec(virt_table.shape, lambda i: (0, 0))],
        out_specs=line,
        out_shape=jax.ShapeDtypeStruct((1, pairs), jnp.float32),
        cost_estimate=pl.CostEstimate(flops=6 * 128 * 288 * pairs, bytes_accessed=200000, transcendentals=0),
    )(occ_index[None, :], virt_index[None, :], occ_table, virt_table)


def halves_kernel(x_lo, coeffs, mine, other, largest):
    for low in range(2):
        @pl.when(x_lo[0] == low)
        def _():
            mine[...] = coeffs[:, low * HALF:(low + 1) * HALF]
            other[...] = coeffs[:, (1 - low) * HALF:(2 - low) * HALF]

    @pl.when(pl.program_id(0) == 0)
    def _():
        largest[...] = jnp.zeros_like(largest)

    top = jnp.zeros((coeffs.shape[0], 128), jnp.float32)
    for c in range(coeffs.shape[1] // 128):
        top = jnp.maximum(top, jnp.abs(coeffs[:, c * 128:(c + 1) * 128].astype(jnp.float32)))
    largest[...] = jnp.maximum(largest[...], jnp.max(top.reshape(-1, 8, 128), axis=0))


def cut_in_halves(x_lo, coeffs):
    half = jax.ShapeDtypeStruct((ROWS, HALF), jnp.bfloat16)
    block = pl.BlockSpec((PART, HALF), lambda i, t: (i, 0))
    return pl.pallas_call(
        halves_kernel,
        grid_spec=pltpu.PrefetchScalarGridSpec(
            num_scalar_prefetch=1,
            grid=(ROWS // PART,),
            in_specs=[pl.BlockSpec((PART, 2 * HALF), lambda i, t: (i, 0))],
            out_specs=[block, block, pl.BlockSpec((8, 128), lambda i, t: (0, 0))],
        ),
        out_shape=[half, half, jax.ShapeDtypeStruct((8, 128), jnp.float32)],
        compiler_params=pltpu.CompilerParams(vmem_limit_bytes=24 * 1024 * 1024),
        cost_estimate=pl.CostEstimate(flops=0, bytes_accessed=PART * ROWS, transcendentals=0),
    )(x_lo[None], coeffs)


def moves(pairs):
    return [(z * 4 + src, (z + dz) % PLANES * 4 + dst) for z in range(PLANES) for src, dst, dz in pairs]


def aux_permute(value, pairs):
    return lax.ppermute(value, "aux", moves(pairs))


def y_permute(value, by):
    return lax.ppermute(value, "pair", [(h * 4 + y, h * 4 + (y + by) % 4) for h in range(2) for y in range(4)])


def x_permute(value, by, roles=range(4)):
    perm = []
    for z in range(PLANES):
        for x in range(4):
            to = (x + by) % 4
            for core in range(2):
                if x % 2 * 2 + core not in roles:
                    continue
                for y in range(4):
                    source = (z * 4 + x % 2 * 2 + core) * 8 + x // 2 * 4 + y
                    perm.append((source, (z * 4 + to % 2 * 2 + core) * 8 + to // 2 * 4 + y))
    return lax.ppermute(value, ("aux", "pair"), perm)


def both_ways(permute, up, down):
    return lax.optimization_barrier((permute(up, 1), permute(down, -1)))


def first_sends(terms, scales):
    return [narrow(terms[0:2], scales), narrow(terms[2:4], scales)]


def second_sends(terms, got, scales):
    return [narrow(terms[6] + wide(got[0][0], scales), scales),
            narrow(terms[7] + wide(got[1][0], scales), scales)]


def finish(terms, got, more, scales, slots=slice(None)):
    zero = terms[4][slots] + wide(got[1][1][slots], scales) + wide(more[0][slots], scales)
    one = terms[5][slots] + wide(got[0][1][slots], scales) + wide(more[1][slots], scales)
    return [zero, one]


def slot_names(role):
    names = []
    for batch in BATCHES:
        names += [(tile, h) for h in range(2) for tile in batch[role]]
    early, late = MOVED[role][:2], MOVED[role][2:]
    names += [(tile, h) for h in range(2) for tile in early]
    names += [(tile, h) for tile in late for h in range(2)]
    return names


def entry_table():
    rows = []
    for role in range(4):
        names = slot_names(role)
        for x_hi in range(2):
            row = []
            for k, d in ORDER:
                to = (x_hi * 2 + role // 2 + k) % 4
                row += [names.index((tile, to // 2)) for tile in ENTRIES[role % 2][to % 2][2 * d:2 * d + 2]]
            rows.append(row)
    return np.array(rows, np.int32)


def pick_kernel(table, slots, parts):
    for i in range(16):
        parts[i] = slots[table[i]]


def pick_parts(table, slots):
    return pl.pallas_call(
        pick_kernel,
        in_specs=[pl.BlockSpec(memory_space=pltpu.SMEM), pl.BlockSpec(memory_space=pltpu.VMEM)],
        out_specs=pl.BlockSpec(memory_space=pltpu.VMEM),
        out_shape=jax.ShapeDtypeStruct((16, PART, ROWS), jnp.float32),
        compiler_params=pltpu.CompilerParams(vmem_limit_bytes=20 * 1024 * 1024),
        cost_estimate=pl.CostEstimate(flops=0, bytes_accessed=PART * ROWS, transcendentals=0),
    )(table, slots)


def largest_round(value, permute):
    got = [permute(value, by) for by in (1, 2, 3)]
    return jnp.maximum(jnp.maximum(value, got[0]), jnp.maximum(got[1], got[2]))


def scales_of(largest):
    bound = 8.0 * HALF * 4 * largest * largest * 4.0
    scale = 32768.0 / jnp.maximum(bound, 1e-30)
    return scale, 1.0 / scale


def narrow(value, scales):
    return (value * scales[0]).astype(jnp.float16)


def wide(value, scales):
    return value.astype(jnp.float32) * scales[1]


def after(value, other):
    return lax.optimization_barrier((value, other))[0]


def local(coeffs, occ_index, virt_index, occ_energy, virt_energy):
    role = lax.rem(lax.axis_index("aux"), 4)
    x_lo = role // 2
    x_hi = lax.axis_index("pair") // 4
    y = lax.rem(lax.axis_index("pair"), 4)

    mine, other, largest = cut_in_halves(x_lo.astype(jnp.int32), coeffs)
    halo_a = aux_permute(mine, [(0, 0, -1), (3, 3, 1)])
    far_a = aux_permute(other, [(0, 2, 0), (3, 1, 0)])
    sib = aux_permute(mine, [(0, 1, 0), (1, 0, 0), (2, 3, 0), (3, 2, 0)])

    largest = jnp.maximum(largest, aux_permute(largest, [(0, 1, 0), (1, 0, 0), (2, 3, 0), (3, 2, 0)]))
    largest = largest_round(largest, y_permute)
    largest = jnp.maximum(largest, x_permute(largest, 2, (1, 2)))
    largest = jnp.maximum(largest, aux_permute(largest, [(1, 2, 0), (2, 1, 0)]))
    largest = jnp.maximum(largest, aux_permute(largest, [(1, 1, 2), (2, 2, 2)]))
    largest = jnp.maximum(largest, aux_permute(largest, [(1, 1, 1), (2, 2, 1)]))
    largest = jnp.maximum(largest, aux_permute(largest, [(1, 0, 0), (2, 3, 0)]))
    scales = scales_of(jnp.max(largest))

    occ_index, virt_index = after([occ_index, virt_index], mine)
    begin = x_lo * HALF
    gap = pair_gaps(
        lax.dynamic_slice_in_dim(occ_index, begin, HALF),
        lax.dynamic_slice_in_dim(virt_index, begin, HALF),
        occ_energy, virt_energy)
    weight = -4.0 * gap / (gap * gap + freq_point * freq_point)

    plans = []
    for batch in BATCHES:
        used = sorted({WHERE[r][t[i:i + 2]] for r in range(4) for t in batch[r] for i in (0, 2)})
        table, held_most = batch_tables(batch, used)
        row = lax.dynamic_index_in_dim(jnp.asarray(table), role, axis=0, keepdims=False)
        row = jnp.concatenate([row, lax.dynamic_index_in_dim(jnp.asarray(ROW_ORDER), y, axis=0, keepdims=False)])
        plans.append([used, row, held_most])
    entries = lax.dynamic_index_in_dim(jnp.asarray(entry_table()), role * 2 + x_hi, axis=0, keepdims=False)
    rows = [plan[1] for plan in plans]
    halo_a, far_a, sib, scales, weight, entries, rows = lax.optimization_barrier(
        (halo_a, far_a, sib, scales, weight, entries, rows))

    far_b = aux_permute(after(other, far_a), [(1, 3, 0), (2, 0, 0)])
    halo_b = aux_permute(after(mine, halo_a), [(1, 1, -1), (2, 2, 1)])
    far_a_sib = aux_permute(far_a, [(1, 0, 0), (2, 3, 0)])
    halo_a_sib = aux_permute(halo_a, [(3, 2, 0)])
    minor = aux_permute(far_a, [(1, 0, 1), (2, 2, -1)])

    held = {OWN: mine, SIB: sib, FAR_A: far_a, HALO_A: halo_a}

    def tiles(number):
        used, _, held_most = plans[number]
        return tile_batch(BATCHES[number], rows[number], held_most, weight, [held[s] for s in used])

    def first_round(sends):
        return [y_permute(sends[0], 1), y_permute(sends[1], -1)]

    partial0 = tiles(0)
    sends0 = first_sends(partial0, scales)
    held[FAR_A_SIB], held[HALO_A_SIB] = after([far_a_sib, halo_a_sib], sends0)
    got0 = first_round(sends0)
    partial1 = tiles(1)
    sends1 = first_sends(partial1, scales)
    got0, sends1 = lax.optimization_barrier((got0, sends1))
    got1 = first_round(sends1)
    more = second_sends(partial0, got0, scales)
    far_b, halo_b, minor, got1, more = lax.optimization_barrier((far_b, halo_b, minor, got1, more))
    held[FAR_B], held[HALO_B], held[MINOR] = far_b, halo_b, minor
    held[FAR_B_SIB] = aux_permute(far_b, [(0, 1, 0), (3, 2, 0)])
    held[HALO_B_SIB] = aux_permute(halo_b, [(2, 3, 0)])
    more = [jnp.concatenate(pair) for pair in zip(more, second_sends(partial1, got1, scales))]
    more = first_round(more)
    partial2 = tiles(2)
    sends2 = first_sends(partial2, scales)
    got2 = first_round(sends2)
    more = after(more, sends2)
    more0, more1 = [m[:2] for m in more], [m[2:] for m in more]
    moved0 = [finish(partial0, got0, more0, scales, slice(1, 2)), finish(partial1, got1, more1, scales, slice(1, 2))]
    moved0 = narrow(jnp.concatenate([tile[h] for h in range(2) for tile in moved0]), scales)
    rows[3], moved0 = lax.optimization_barrier((rows[3], moved0, sends2))[:2]
    moved0 = aux_permute(moved0, [(0, 0, 1)])
    partial3 = tiles(3)
    sends3 = first_sends(partial3, scales)
    got2, moved0 = lax.optimization_barrier((got2, moved0, partial3))[:2]
    sends2 = second_sends(partial2, got2, scales)
    more2 = first_round(sends2)
    sends3 = after(sends3, sends2)
    got3 = first_round(sends3)
    more2 = after(more2, sends3)
    total2 = finish(partial2, got2, more2, scales)
    moved2 = [narrow(jnp.stack([total2[0][i], total2[1][i]]), scales) for i in range(2)]
    more0, more1 = after([more0, more1], moved2)
    total0 = finish(partial0, got0, more0, scales)
    total1 = finish(partial1, got1, more1, scales)
    moved2 = [aux_permute(moved2[0], [(0, 0, 1), (1, 1, 1), (2, 2, 1)]), aux_permute(moved2[1], [(1, 1, 1)])]
    got3, moved2 = lax.optimization_barrier((got3, moved2))
    more3 = both_ways(y_permute, *second_sends(partial3, got3, scales))
    moved0, moved2 = wide(moved0, scales), wide(jnp.concatenate(moved2), scales)
    total3 = finish(partial3, got3, more3, scales)
    slots = jnp.concatenate(total0 + total1 + total2 + total3 + [moved0, moved2])
    terms = pick_parts(entries, slots).reshape(8, 2, PART, ROWS)
    got = both_ways(x_permute, *first_sends(terms, scales))
    zero, one = finish(terms, got, both_ways(x_permute, *second_sends(terms, got, scales)), scales)
    final = [zero[0], zero[1], one[0], one[1]]

    crossed = narrow(jnp.stack(final[1:]), scales).reshape(3, PART, 8, PART)
    crossed = lax.all_to_all(crossed, "pair", split_axis=2, concat_axis=1, tiled=True)
    crossed = crossed.reshape(3, ROWS, PART)

    swapped = aux_permute(after(narrow(one[0], scales), crossed), [(2, 3, 0), (3, 2, 0)])
    lower = [final[0], final[1], jnp.where(x_lo == 1, wide(swapped, scales), final[2]), final[3]]

    back = [
        [(0, 3, -1), (1, 0, 0), (2, 1, 0), (3, 2, 0)],
        [(0, 2, -1), (1, 3, -1), (2, 1, 0), (3, 0, 0)],
        [(0, 1, -1), (1, 2, -1), (2, 3, -1), (3, 0, 0)],
    ]
    upper = [wide(aux_permute(crossed[o], back[o]), scales).T for o in range(3)]
    return jnp.stack(lower[::-1] + upper)


def solution(mesh):
    return jax.shard_map(
        local,
        mesh=mesh,
        in_specs=(P("aux", "pair"), P("pair"), P("pair"), P(), P()),
        out_specs=P(None, ("aux", "pair"), None),
        check_vma=False,
    )
```
